256 devices in a mesh: tm: 32 (over z, y), clip: 8 (over x, core).
Axes of the slice: x: 4, y: 4, z: 8, core: 2. Of those that a mesh axis runs over, the one named last changes fastest.
Arguments:
- block_input: bfloat16 [8, 128, 16, 16, 256], P('clip', 'tm'), may hold values from -6 to 6
- pre_act: bfloat16 [8, 128, 16, 16, 512], P('clip', 'tm'), may hold values from -6 to 6
- time_out: bfloat16 [8, 128, 16, 16, 512], P('clip', 'tm'), may hold values from -6 to 6
- w_space: bfloat16 [256, 3, 3, 512], replicated, may hold values from -0.125 to 0.125
- w_time: bfloat16 [512, 3, 512], replicated, may hold values from -0.15625 to 0.15625
- proj: bfloat16 [512, 18], replicated, may hold values from -0.25 to 0.25
- codes: int32 [8, 128, 16, 16], P('clip', 'tm'), may hold values from 0 to 262143
- cotan: bfloat16 [8, 128, 16, 16, 18], P('clip', 'tm'), may hold values from -6 to 6
- lengths: int32 [8], replicated, may hold values from 1 to 128
Outputs:
- grad_input: bfloat16 [8, 128, 256, 256], P('clip', None, 'tm')
- grad_space: float32 [256, 3, 3, 512], P('tm')
- grad_time: float32 [512, 3, 512], P('tm')
- grad_proj: float32 [512, 18], P('tm')
The draws below stay inside these ranges and needn't reach their ends.
All inputs are finite; a program needn't handle non-finite values.
Results may differ from the reference program's by a relative error of at most 0.025.
Values may be sent and summed in bfloat16 or wider, within the bound.
A program may use at most 64 MiB of HBM per device.

```python
import math
import jax
import jax.numpy as jnp
from jax import lax

CIN = 256
CMID = 512
LATENT = 18
SIDE = 16
FRAMES = 128
CLIPS = 8


def place_ends(array, own_key, smallest, high):
    place = [jax.random.randint(jax.random.fold_in(own_key, axis), (), 0, length) for axis, length in enumerate(array.shape)]
    longest = array.shape.index(max(array.shape))
    neighbour = place[:longest] + [(place[longest] + 1) % array.shape[longest]] + place[longest + 1:]
    return array.at[tuple(place)].set(smallest).at[tuple(neighbour)].set(high)


def with_spikes(array, rng, source, target, parts, factor):
    owner, partner = [(jnp.arange(array.shape[position]) // (array.shape[position] // parts)).reshape([-1 if axis == position else 1 for axis in range(array.ndim)]) for position in (source, target)]
    chosen = jax.random.permutation(rng, parts)[partner]
    strong = (owner == chosen) | (owner == (partner + parts // 2) % parts)
    return jnp.where(strong, factor * array, array)


def level_of(stream_key, dims, shards, low, largest):
    loudness = 1.0
    for position, parts in shards:
        heights = jax.random.uniform(jax.random.fold_in(jax.random.fold_in(stream_key, 6), position), (parts,), jnp.float32, low / len(shards), largest / len(shards))
        loudness = loudness * jnp.repeat(jnp.exp(heights), dims[position] // parts).reshape((-1,) + (1,) * (len(dims) - 1 - position))
    return loudness


def scatter_about(own_key, shape, spread, limit, pieces=(), dtype=jnp.bfloat16):
    result = spread * jax.random.normal(own_key, shape, jnp.float32)
    if pieces:
        result = result * level_of(own_key, shape, pieces, -0.22, 0.18)
    return jnp.clip(result, -limit, limit).astype(dtype)


def noise_with(stream_key, shape, deviation, reach, pieces, heavy, held_as=jnp.bfloat16):
    array = deviation * jax.random.normal(stream_key, shape, jnp.float32)
    if pieces:
        array = array * level_of(stream_key, shape, pieces, -0.22, 0.18)
    return jnp.clip(with_spikes(array, jax.random.fold_in(stream_key, 3), *heavy), -reach, reach).astype(held_as)


def setup_inputs(seed: int = 0) -> dict:
    key_list = jax.random.split(jax.random.key(seed), 10)
    block_input = noise_with(key_list[0], (CLIPS, FRAMES, SIDE, SIDE, CIN), 1.0, 6.0, ((0, 8), (1, 32)), (1, 4, 32, 2.75))
    pre_act = noise_with(key_list[1], (CLIPS, FRAMES, SIDE, SIDE, CMID), 1.0, 6.0, ((0, 8), (1, 32)), (1, 4, 32, 2.75))
    time_out = noise_with(key_list[2], (CLIPS, FRAMES, SIDE, SIDE, CMID), 1.0, 6.0, ((0, 8), (1, 32)), (1, 4, 32, 2.75))
    w_space = scatter_about(key_list[3], (CIN, 3, 3, CMID), (9 * CIN) ** -0.5, 0.125)
    w_time = scatter_about(key_list[4], (CMID, 3, CMID), (3 * CMID) ** -0.5, 0.15625)
    proj = scatter_about(key_list[5], (CMID, LATENT), CMID ** -0.5, 0.25)
    codes = place_ends(jax.random.randint(key_list[6], (CLIPS, FRAMES, SIDE, SIDE), 0, 262144), jax.random.fold_in(key_list[6], 1), 0, 262143).astype(jnp.int32)
    cotan = scatter_about(key_list[7], (CLIPS, FRAMES, SIDE, SIDE, LATENT), 1.0, 6.0, ((0, 8), (1, 32)))
    lengths = place_ends(jax.random.randint(key_list[8], (CLIPS,), 1, FRAMES + 1), jax.random.fold_in(key_list[8], 1), 1, FRAMES).astype(jnp.int32)
    return dict(block_input=block_input, pre_act=pre_act, time_out=time_out, w_space=w_space, w_time=w_time, proj=proj, codes=codes, cotan=cotan, lengths=lengths)


commit_weight = 0.25

def shift_space(values, down, right):
    side_len = values.shape[-2]
    padded = jnp.pad(values, ((0, 0), (1, 1), (1, 1), (0, 0)))
    return padded[:, 1 + down:1 + down + side_len, 1 + right:1 + right + side_len, :]

def silu_slope(pre):
    sigma = jax.nn.sigmoid(pre)
    return sigma * (1.0 + pre * (1.0 - sigma))

def sign_targets(flat_codes, latent):
    powers = (2 ** jnp.arange(latent)).astype(jnp.int32)
    bits = flat_codes[:, None] // powers[None, :] % 2
    return 2.0 * bits.astype(jnp.float32) - 1.0

def reference(block_input, pre_act, time_out, w_space, w_time, proj, codes, cotan, lengths):
    clips, frames, side_len, _, cin = block_input.shape
    cmid = pre_act.shape[-1]
    latent = proj.shape[1]
    positions = side_len * side_len
    rows = frames * positions
    scale = 1.0 / math.sqrt(clips * rows)

    def one_clip(packed):
        clip_x, clip_pre, clip_t, clip_codes, clip_cot, clip_len = packed
        t_rows = clip_t.reshape(rows, cmid)
        latent_z = jnp.dot(t_rows, proj, preferred_element_type=jnp.float32)
        targets = sign_targets(clip_codes.reshape(rows), latent)
        live = (jnp.arange(frames) < clip_len).astype(jnp.float32)
        live_rows = jnp.repeat(live, positions)[:, None]
        grad_z = (live_rows * (clip_cot.reshape(rows, latent).astype(jnp.float32) + 2.0 * commit_weight * (latent_z - targets))).astype(jnp.bfloat16)
        proj_part = jnp.dot(t_rows.T, grad_z, preferred_element_type=jnp.float32)
        grad_t = jnp.dot(grad_z, proj.T, preferred_element_type=jnp.float32).astype(jnp.bfloat16)
        grad_t = grad_t.reshape(frames, positions, cmid)
        act = jax.nn.silu(clip_pre.astype(jnp.float32)).astype(jnp.bfloat16).reshape(frames, positions, cmid)
        zero_two = jnp.zeros((2, positions, cmid), jnp.bfloat16)
        t_ext = jnp.concatenate([grad_t, zero_two], axis=0)
        a_ext = jnp.concatenate([zero_two, act], axis=0)
        grad_t_rows = grad_t.reshape(rows, cmid)
        grad_act = jnp.zeros((rows, cmid), jnp.float32)
        time_terms = []
        for lag in range(3):
            ahead = t_ext[lag:lag + frames].reshape(rows, cmid)
            grad_act = grad_act + jnp.dot(ahead, w_time[:, lag, :].T, preferred_element_type=jnp.float32)
            behind = a_ext[2 - lag:2 - lag + frames].reshape(rows, cmid)
            time_terms.append(jnp.dot(behind.T, grad_t_rows, preferred_element_type=jnp.float32))
        time_part = jnp.stack(time_terms, axis=1)
        grad_pre = (grad_act.reshape(frames, side_len, side_len, cmid) * silu_slope(clip_pre.astype(jnp.float32))).astype(jnp.bfloat16)
        pre_rows = grad_pre.reshape(rows, cmid)
        grad_x = jnp.zeros((frames, side_len, side_len, cin), jnp.float32)
        space_rows = []
        for row_tap in range(3):
            row_terms = []
            for col_tap in range(3):
                moved = shift_space(clip_x, row_tap - 1, col_tap - 1).reshape(rows, cin)
                row_terms.append(jnp.dot(moved.T, pre_rows, preferred_element_type=jnp.float32))
                back = jnp.dot(pre_rows, w_space[:, row_tap, col_tap, :].T, preferred_element_type=jnp.float32)
                grad_x = grad_x + shift_space(back.reshape(frames, side_len, side_len, cin), 1 - row_tap, 1 - col_tap)
            space_rows.append(jnp.stack(row_terms, axis=1))
        space_part = jnp.stack(space_rows, axis=1)
        return (grad_x.astype(jnp.bfloat16).reshape(frames, positions, cin), space_part, time_part, proj_part)
    results = lax.map(one_clip, (block_input, pre_act, time_out, codes, cotan, lengths))
    grad_input = results[0]
    grad_space = lax.optimization_barrier(jnp.sum(results[1], axis=0)) * scale
    grad_time = lax.optimization_barrier(jnp.sum(results[2], axis=0)) * scale
    grad_proj = lax.optimization_barrier(jnp.sum(results[3], axis=0)) * scale
    return (grad_input, grad_space, grad_time, grad_proj)
```

```python
import jax
import jax.numpy as jnp
from jax import lax
from jax.experimental import pallas as pl
from jax.experimental.pallas import tpu as pltpu
from jax.sharding import PartitionSpec as P

MESH = pl.DeviceIdType.MESH
F32 = jnp.float32
BF16 = jnp.bfloat16
I32 = jnp.int32

NZ, NY, NX, NC = 8, 4, 4, 2
NT, NG = NZ * NY, NX * NC
FR, CELLS, CIN, CMID, LAT = 4, 256, 256, 512, 18
ROWS = FR * CELLS
PAIR = 2 * CELLS
SCALE = 1.0 / 512.0

NT_DIMS = (((1,), (1,)), ((), ()))
TN_DIMS = (((0,), (0,)), ((), ()))


def iota(shape, dim):
    return lax.broadcasted_iota(I32, shape, dim)


def ones_where(cond):
    return jnp.where(cond, 1.0, 0.0).astype(BF16)


def dot(a, b):
    return jnp.dot(a, b, preferred_element_type=F32)


def dot_nt(a, b):
    return lax.dot_general(a, b, NT_DIMS, preferred_element_type=F32)


def dot_tn(a, b):
    return lax.dot_general(a, b, TN_DIMS, preferred_element_type=F32)


def kernel(
    x_hbm, pre_hbm, t_hbm, ws_hbm, wt_hbm, pj_hbm, codes_hbm, cot_hbm, len_ref,
    out_hbm, space_ref, time_ref, proj_ref,
    x_v, pre_v, t_v, ws_v, wt_v, pj_v, codes_v, cot_v,
    p3_v, gz_v, zc_v, mt_v, act_v, slope_v, g3_v, xt_v,
    halo_s, halo_r, ab_v,
    pw1, pw2, rc1, rc2,
    rel1, rel2, sum1, sum2, fin1, fin2,
    yb, ry, zs, rz, fs, ra,
    in_sem, halo_ss, halo_rs, a2a_ss, a2a_rs,
    core_ss, core_rs, x_ss, x_rs, y_ss, y_rs, z_ss, z_rs, g_ss, g_rs,
):
    tm = lax.axis_index("tm")
    clip = lax.axis_index("clip")
    z, y = tm // NY, tm % NY
    x, core = clip // NC, clip % NC

    def load(src, dst, i):
        copy = pltpu.make_async_copy(src, dst, in_sem.at[i])
        copy.start()
        return copy

    ld_pj = load(pj_hbm, pj_v, 0)
    ld_t0 = load(t_hbm.at[pl.ds(0, PAIR)], t_v.at[pl.ds(0, PAIR)], 1)
    ld_cd = load(codes_hbm, codes_v, 2)
    ld_ct = load(cot_hbm, cot_v, 3)
    ld_t1 = load(t_hbm.at[pl.ds(PAIR, PAIR)], t_v.at[pl.ds(PAIR, PAIR)], 4)
    ld_wt = load(wt_hbm, wt_v, 5)
    ld_pre = load(pre_hbm, pre_v, 6)
    ld_x = load(x_hbm, x_v, 7)
    ld_ws = load(ws_hbm, ws_v, 8)

    barrier = pltpu.get_barrier_semaphore()

    @pl.loop(1, NT)
    def _(d):
        pl.semaphore_signal(
            barrier, inc=1, device_id=(lax.rem(tm + d, NT), clip), device_id_type=MESH
        )

    @pl.loop(1, NG)
    def _(d):
        pl.semaphore_signal(
            barrier, inc=1, device_id=(tm, lax.rem(clip + d, NG)), device_id_type=MESH
        )

    ld_pj.wait()
    row_l = iota((128, LAT), 0) % 32
    rep = ones_where(row_l == iota((128, LAT), 1))
    p3_v[...] = dot(rep, pj_v[...]).astype(BF16)

    rep_t = ones_where(iota((LAT, 128), 0) == iota((LAT, 128), 1) % 32)
    lane = iota((PAIR, 128), 1)
    lane_l = lane % 32
    row_id = iota((PAIR, 128), 0)
    spread = ones_where(iota((PAIR, 32), 0) // 16 == iota((PAIR, 32), 1))
    pick = ones_where(
        (iota((128, 128), 0) // 16 == (iota((128, 128), 1) % 32) // 6)
        & (iota((128, 128), 1) % 32 < LAT)
    )
    clip_len = len_ref[clip]

    def latents(fp):
        rows = pl.ds(fp * PAIR, PAIR)
        lat = dot_nt(t_v[rows, :], p3_v[...])
        cot = dot(cot_v[rows, :], rep_t)
        cd = codes_v[pl.ds(fp * 32, 32), :]
        packed = jnp.zeros((32, 128), F32)
        for piece in range(3):
            part = ((cd >> (6 * piece)) & 63).astype(F32).astype(BF16)
            place = ones_where(iota((16, 128), 1) == iota((16, 128), 0) + 16 * piece)
            packed = packed + dot(part, place)
        wide = dot(spread, packed.astype(BF16))
        own = jnp.where((lane < 48) & (lane % 16 == row_id % 16), wide, 0.0)
        six = dot(own.astype(BF16), pick).astype(I32)
        bit = (six >> (lane_l % 6)) & 1
        target = (2 * bit - 1).astype(F32)
        frame = tm * FR + fp * 2 + row_id // CELLS
        keep = (frame < clip_len) & (lane_l < LAT)
        grad = jnp.where(keep, cot + 0.5 * (lat - target), 0.0)
        gz_v[rows, :] = grad.astype(BF16)

    ld_t0.wait()
    ld_cd.wait()
    ld_ct.wait()
    latents(0)

    group = iota((CELLS, 128), 1) // 32

    def gz(f):
        return gz_v[f * CELLS : (f + 1) * CELLS, :].astype(F32)

    halo_s[...] = jnp.where(
        group == 0, 0.0, jnp.where(group == 2, gz(1), gz(0))
    ).astype(BF16)
    pl.semaphore_wait(barrier, NT - 1 + NG - 1)
    halo = pltpu.make_async_remote_copy(
        src_ref=halo_s, dst_ref=halo_r, send_sem=halo_ss, recv_sem=halo_rs,
        device_id=(lax.rem(tm + NT - 1, NT), clip), device_id_type=MESH,
    )
    halo.start()

    ld_t1.wait()
    latents(1)
    zc_v[0:CELLS, :] = jnp.where(
        group == 0, gz(0), jnp.where(group == 1, gz(1), jnp.where(group == 2, gz(2), 0.0))
    ).astype(BF16)
    zc_v[CELLS:PAIR, :] = jnp.where(
        group == 0, gz(1), jnp.where(group == 1, gz(2), jnp.where(group == 2, gz(3), 0.0))
    ).astype(BF16)

    ld_wt.wait()
    for k in range(3):
        folded = dot_nt(p3_v[0:32, :], wt_v[k]).astype(BF16)
        mt_v[32 * k : 32 * k + 32, :] = folded
        if k == 2:
            mt_v[96:128, :] = folded

    ld_pre.wait()

    @pl.loop(0, ROWS // 64)
    def _(i):
        rows = pl.ds(pl.multiple_of(i * 64, 64), 64)
        v = pre_v[rows, :].astype(F32)
        s = 0.5 * jnp.tanh(0.5 * v) + 0.5
        a = v * s
        act_v[rows, :] = a.astype(BF16)
        slope_v[rows, :] = s + a * (1.0 - s)

    zero16 = jnp.zeros((16, CMID), BF16)

    def grad_pre(f):
        lo, hi = f * CELLS, (f + 1) * CELLS
        g = (dot(zc_v[lo:hi, :], mt_v[...]) * slope_v[lo:hi, :]).astype(BF16)
        g3_v[1, lo:hi, :] = g
        g3_v[0, lo : hi - 16, :] = g[16:]
        g3_v[0, hi - 16 : hi, :] = zero16
        g3_v[2, lo + 16 : hi, :] = g[: CELLS - 16]
        g3_v[2, lo : lo + 16, :] = zero16

    row_p = iota((PAIR, CIN), 0) % 16

    def grad_x(fp):
        rows = slice(fp * PAIR, (fp + 1) * PAIR)
        back = []
        for b in range(3):
            acc = dot_nt(g3_v[0, rows, :], ws_v[b])
            for a in range(1, 3):
                acc = acc + dot_nt(g3_v[a, rows, :], ws_v[3 * a + b])
            back.append(acc)
        g = (
            back[1]
            + jnp.where(row_p != 15, pltpu.roll(back[0], PAIR - 1, 0), 0.0)
            + jnp.where(row_p != 0, pltpu.roll(back[2], 1, 0), 0.0)
        )
        for t in range(NT):
            both = jnp.concatenate(
                [g[8 * t : 8 * t + 8], g[CELLS + 8 * t : CELLS + 8 * t + 8]], axis=0
            )
            ab_v[t, fp] = both.astype(BF16)

        @pl.loop(1, NT)
        def _(d):
            to = lax.rem(tm + d, NT)
            pltpu.make_async_remote_copy(
                src_ref=ab_v.at[to, fp], dst_ref=out_hbm.at[2 * tm + fp],
                send_sem=a2a_ss, recv_sem=a2a_rs,
                device_id=(to, clip), device_id_type=MESH,
            ).start()

        pltpu.make_async_copy(ab_v.at[tm, fp], out_hbm.at[2 * tm + fp], a2a_rs).start()

    grad_pre(0)
    grad_pre(1)
    ld_ws.wait()
    grad_x(0)

    ld_x.wait()
    r = iota((CIN, CIN), 0)
    c = iota((CIN, CIN), 1)
    perm = ones_where(
        c == (r // 16) % 4 * 64 + (r // 8) % 2 * 32 + r // 64 * 8 + r % 8
    )
    shift_lo = ones_where((r == c - 1) & (c % 16 != 0))
    shift_hi = ones_where((r == c + 1) & (c % 16 != 15))
    for f in range(FR):
        lo, hi = f * CELLS, (f + 1) * CELLS
        xt = dot_nt(perm, x_v[lo:hi, :]).astype(BF16)
        xt_v[256:512, lo:hi] = xt
        xt_v[0:256, lo:hi] = dot(xt, shift_lo).astype(BF16)
        xt_v[512:768, lo:hi] = dot(xt, shift_hi).astype(BF16)

    halo.wait_recv()
    ahead = jnp.where(tm == NT - 1, 0.0, halo_r[...].astype(F32))
    zc_v[PAIR : PAIR + CELLS, :] = jnp.where(
        group == 0, gz(2), jnp.where(group == 1, gz(3), jnp.where(group == 3, ahead, 0.0))
    ).astype(BF16)
    zc_v[PAIR + CELLS :, :] = jnp.where(
        group == 0, gz(3), jnp.where(group == 3, 0.0, ahead)
    ).astype(BF16)
    grad_pre(2)
    grad_pre(3)

    gt = dot_tn(zc_v[...], act_v[...])
    pt = dot_tn(gz_v[...], t_v[...])
    q_t = jnp.concatenate([gt[0:64], gt[64:96] + gt[96:128], pt[96:128]], axis=0)
    q = q_t.T
    for cc in range(NC):
        for yy in range(NY):
            for zp in range(NZ // 2):
                lo = 16 * (2 * zp * NY + yy) + 8 * cc
                hi = 16 * ((2 * zp + 1) * NY + yy) + 8 * cc
                tile = jnp.concatenate([q[lo : lo + 8], q[hi : hi + 8]], axis=0).astype(BF16)
                at = yy * 64 + zp * 16
                pw2[cc, 3, 0, at : at + 16, :] = tile
                pw2[cc, 3, 1, at : at + 16, :] = tile

    def space(a, half):
        cols = pl.ds(pl.multiple_of(half * 256, 256), 256)
        acc = dot(xt_v[...], g3_v[a, :, cols])
        for b in range(3):
            for lb in range(2):
                block = acc[256 * b : 256 * b + 256, 128 * lb : 128 * lb + 128].astype(BF16)
                if a < 2:
                    i = 6 * a + 2 * b + lb
                    pw1[half, i // 3, i % 3] = block
                else:
                    i = 2 * b + lb
                    pw2[half, i // 2, i % 2] = block

    other = 1 - core
    mate = (tm, x * NC + other)

    def core_copy(src, dst, i):
        return pltpu.make_async_remote_copy(
            src_ref=src, dst_ref=dst, send_sem=core_ss.at[i], recv_sem=core_rs.at[i],
            device_id=mate, device_id_type=MESH,
        )

    core_copies = (
        core_copy(pw1.at[other, pl.ds(0, 2)], rc1.at[pl.ds(0, 2)], 0),
        core_copy(pw1.at[other, pl.ds(2, 2)], rc1.at[pl.ds(2, 2)], 1),
        core_copy(pw2.at[other], rc2, 2),
    )
    for a in range(3):
        space(a, other)
        core_copies[a].start()
    for a in range(3):
        space(a, core)

    left, right, far = lax.rem(x + 3, NX), lax.rem(x + 1, NX), lax.rem(x + 2, NX)

    def x_copy(src, dst, to, i):
        return pltpu.make_async_remote_copy(
            src_ref=src, dst_ref=dst, send_sem=x_ss.at[i], recv_sem=x_rs.at[i],
            device_id=(tm, to * NC + core), device_id_type=MESH,
        )

    half_a, half_b = pl.ds(0, 128), pl.ds(128, 128)

    def x_first(w, pw, rc, rel, sm, fin):
        def add(chunk):
            for s in range(pw.shape[2]):
                sm[chunk, s] = (pw[core, chunk, s].astype(F32) + rc[chunk, s].astype(F32)).astype(BF16)

        add(far)
        to_l = x_copy(sm.at[far, :, half_a], rel.at[0], left, w + 0)
        to_r = x_copy(sm.at[far, :, half_b], rel.at[1], right, w + 1)
        to_l.start()
        to_r.start()
        add(left)
        d_l = x_copy(sm.at[left, :, half_b], fin.at[1, :, half_b], left, w + 2)
        d_l.start()
        add(right)
        d_r = x_copy(sm.at[right, :, half_a], fin.at[0, :, half_a], right, w + 3)
        d_r.start()
        add(x)
        return [to_l, to_r, d_l, d_r]

    def x_second(w, rel, sm, fin, copies):
        n = sm.shape[1]
        copies[0].wait_recv()
        for s in range(n):
            sm[left, s, 0:128] = (sm[left, s, 0:128].astype(F32) + rel[0, s].astype(F32)).astype(BF16)
        s_l = x_copy(sm.at[left, :, half_a], fin.at[1, :, half_a], left, w + 4)
        s_l.start()
        copies[1].wait_recv()
        for s in range(n):
            sm[right, s, 128:256] = (sm[right, s, 128:256].astype(F32) + rel[1, s].astype(F32)).astype(BF16)
        s_r = x_copy(sm.at[right, :, half_b], fin.at[0, :, half_b], right, w + 5)
        s_r.start()
        return [s_l, s_r]

    core_copies[0].wait_recv()
    core_copies[1].wait_recv()
    first1 = x_first(0, pw1, rc1, rel1, sum1, fin1)
    core_copies[2].wait_recv()
    first2 = x_first(6, pw2, rc2, rel2, sum2, fin2)

    grad_x(1)

    second1 = x_second(0, rel1, sum1, fin1, first1)
    second2 = x_second(6, rel2, sum2, fin2, first2)

    def x_last(sm, fin, first, second, base):
        for copy in first[2:] + second:
            copy.wait_recv()
        for s in range(sm.shape[1]):
            tot = sm[x, s].astype(F32) + fin[0, s].astype(F32) + fin[1, s].astype(F32)
            tot = tot.astype(BF16)
            for yy in range(NY):
                yb[yy, base + s] = tot[64 * yy : 64 * yy + 64]

    x_last(sum1, fin1, first1, second1, 0)
    x_last(sum2, fin2, first2, second2, 3)

    y_copies = []
    for d in range(1, NY):
        to = lax.rem(y + d, NY)
        copy = pltpu.make_async_remote_copy(
            src_ref=yb.at[to], dst_ref=ry.at[d - 1],
            send_sem=y_ss.at[d - 1], recv_sem=y_rs.at[d - 1],
            device_id=(z * NY + to, clip), device_id_type=MESH,
        )
        copy.start()
        y_copies.append(copy)
    for copy in y_copies:
        copy.wait_recv()
    tots = []
    for s in range(5):
        tot = yb[y, s].astype(F32)
        for d in range(NY - 1):
            tot = tot + ry[d, s].astype(F32)
        tots.append(tot)
    blank = jnp.zeros((8, 128), F32)
    for zz in range(NZ):
        eights = [tot[8 * zz : 8 * zz + 8] for tot in tots] + [blank]
        for i in range(3):
            zs[zz, 16 * i : 16 * i + 16] = jnp.concatenate(
                eights[2 * i : 2 * i + 2], axis=0
            ).astype(BF16)

    z_copies = []
    for d in range(1, NZ):
        to = lax.rem(z + d, NZ)
        copy = pltpu.make_async_remote_copy(
            src_ref=zs.at[to], dst_ref=rz.at[d - 1],
            send_sem=z_ss.at[d - 1], recv_sem=z_rs.at[d - 1],
            device_id=(to * NY + y, clip), device_id_type=MESH,
        )
        copy.start()
        z_copies.append(copy)
    for copy in z_copies:
        copy.wait_recv()
    tot = zs[z].astype(F32)
    for d in range(NZ - 1):
        tot = tot + rz[d].astype(F32)
    fs[...] = (tot * SCALE).astype(BF16)
    ra[clip] = fs[...]

    g_copies = []
    for d in range(1, NG):
        copy = pltpu.make_async_remote_copy(
            src_ref=fs, dst_ref=ra.at[clip],
            send_sem=g_ss.at[d - 1], recv_sem=g_rs.at[d - 1],
            device_id=(tm, lax.rem(clip + d, NG)), device_id_type=MESH,
        )
        copy.start()
        g_copies.append(copy)
    for copy in g_copies:
        copy.wait_recv()

    for cc in range(NC):
        for i in range(18):
            a, b, lb = i // 6, i // 2 % 3, i % 2
            if a < 2:
                xx, s = i // 3, i % 3
            else:
                xx, s = (i - 12) // 2, 3 + i % 2
            tile = ra[xx * NC + cc, 16 * (s // 2) : 16 * (s // 2) + 16].astype(F32)
            lo = 256 * cc + 128 * lb
            space_ref[3 * a + b, :, lo : lo + 128] = tile[8 * (s % 2) : 8 * (s % 2) + 8]
    qs = jnp.concatenate([ra[3 * NC + cc, 16:32].astype(F32)[8:16] for cc in range(NC)], axis=0)
    q_lane = iota((16, 128), 1)
    for k in range(3):
        time_ref[k] = dot(jnp.where(q_lane // 32 == k, qs, 0.0).astype(BF16), p3_v[...])
    take = ones_where(iota((128, LAT), 0) == iota((128, LAT), 1) + 96)
    proj_ref[...] = dot(qs.astype(BF16), take)

    halo.wait_send()
    for copy in core_copies:
        copy.wait_send()
    for copy in first1 + first2 + second1 + second2 + y_copies + z_copies + g_copies:
        copy.wait_send()
    sent = ab_v.at[pl.ds(0, NT - 1)]
    pltpu.make_async_copy(sent, sent, a2a_ss).wait()
    pltpu.make_async_copy(out_hbm, out_hbm, a2a_rs).wait()


def per_device(block_input, pre_act, time_out, w_space, w_time, proj, codes, cotan, lengths):
    args = (
        block_input.reshape(ROWS, CIN),
        pre_act.reshape(ROWS, CMID),
        time_out.reshape(ROWS, CMID),
        w_space.transpose(1, 2, 0, 3).reshape(9, CIN, CMID),
        w_time.transpose(1, 0, 2),
        proj.T,
        codes.reshape(FR * 16, 16),
        cotan.reshape(ROWS, LAT),
        lengths,
    )
    anywhere = pl.BlockSpec(memory_space=pl.ANY)
    vmem = pl.BlockSpec(memory_space=pltpu.VMEM)
    dma = pltpu.SemaphoreType.DMA
    v = pltpu.VMEM
    out, space, time, projg = pl.pallas_call(
        kernel,
        out_shape=(
            jax.ShapeDtypeStruct((2 * NT, 16, CIN), BF16),
            jax.ShapeDtypeStruct((9, 8, CMID), F32),
            jax.ShapeDtypeStruct((3, 16, CMID), F32),
            jax.ShapeDtypeStruct((16, LAT), F32),
        ),
        in_specs=[anywhere] * 8 + [pl.BlockSpec(memory_space=pltpu.SMEM)],
        out_specs=(anywhere, vmem, vmem, vmem),
        scratch_shapes=[
            v((ROWS, CIN), BF16), v((ROWS, CMID), BF16), v((ROWS, CMID), BF16),
            v((9, CIN, CMID), BF16), v((3, CMID, CMID), BF16), v((LAT, CMID), BF16),
            v((FR * 16, 16), I32), v((ROWS, LAT), BF16),
            v((128, CMID), BF16), v((ROWS, 128), BF16), v((ROWS, 128), BF16),
            v((128, CMID), BF16), v((ROWS, CMID), BF16), v((ROWS, CMID), F32),
            v((3, ROWS, CMID), BF16), v((768, ROWS), BF16),
            v((CELLS, 128), BF16), v((CELLS, 128), BF16), v((NT, 2, 16, CIN), BF16),
            v((NC, NX, 3, 256, 128), BF16), v((NC, NX, 2, 256, 128), BF16),
            v((NX, 3, 256, 128), BF16), v((NX, 2, 256, 128), BF16),
            v((2, 3, 128, 128), BF16), v((2, 2, 128, 128), BF16),
            v((NX, 3, 256, 128), BF16), v((NX, 2, 256, 128), BF16),
            v((2, 3, 256, 128), BF16), v((2, 2, 256, 128), BF16),
            v((NY, 5, 64, 128), BF16), v((NY - 1, 5, 64, 128), BF16),
            v((NZ, 48, 128), BF16), v((NZ - 1, 48, 128), BF16),
            v((48, 128), BF16), v((NG, 48, 128), BF16),
            dma((9,)), dma(()), dma(()), dma(()), dma(()),
            dma((3,)), dma((3,)), dma((12,)), dma((12,)),
            dma((NY - 1,)), dma((NY - 1,)), dma((NZ - 1,)), dma((NZ - 1,)),
            dma((NG - 1,)), dma((NG - 1,)),
        ],
        compiler_params=pltpu.CompilerParams(
            collective_id=0, has_side_effects=True, vmem_limit_bytes=56 * 1024 * 1024
        ),
    )(*args)
    return (
        out.reshape(1, FR * NT, 8, CIN),
        space.reshape(3, 3, 8, CMID).transpose(2, 0, 1, 3),
        time.transpose(1, 0, 2),
        projg,
    )


def solution(mesh):
    placed = (
        P("clip", "tm", None, None, None),
        P("clip", "tm", None, None, None),
        P("clip", "tm", None, None, None),
        P(),
        P(),
        P(),
        P("clip", "tm", None, None),
        P("clip", "tm", None, None, None),
        P(),
    )
    return jax.shard_map(
        per_device,
        mesh=mesh,
        in_specs=placed,
        out_specs=(
            P("clip", None, "tm", None),
            P("tm", None, None, None),
            P("tm", None, None),
            P("tm", None),
        ),
        check_vma=False,
    )
```

```python
import jax
import jax.numpy as jnp
from jax import lax
from jax.experimental import pallas as pl
from jax.experimental.pallas import tpu as pltpu
from jax.sharding import PartitionSpec as P

MESH = pl.DeviceIdType.MESH
F32 = jnp.float32
BF16 = jnp.bfloat16
I32 = jnp.int32

NZ, NY, NX, NC = 8, 4, 4, 2
NT, NG = NZ * NY, NX * NC
FR, CELLS, CIN, CMID, LAT = 4, 256, 256, 512, 18
ROWS = FR * CELLS
PAIR = 2 * CELLS
SCALE = 1.0 / 512.0

NT_DIMS = (((1,), (1,)), ((), ()))
TN_DIMS = (((0,), (0,)), ((), ()))


def iota(shape, dim):
    return lax.broadcasted_iota(I32, shape, dim)


def ones_where(cond):
    return jnp.where(cond, 1.0, 0.0).astype(BF16)


def dot(a, b):
    return jnp.dot(a, b, preferred_element_type=F32)


def dot_nt(a, b):
    return lax.dot_general(a, b, NT_DIMS, preferred_element_type=F32)


def dot_tn(a, b):
    return lax.dot_general(a, b, TN_DIMS, preferred_element_type=F32)


def kernel(
    x_hbm, pre_hbm, t_hbm, ws_hbm, wt_hbm, pj_hbm, codes_hbm, cot_hbm, len_hbm,
    out_hbm, ra,
    x_v, pre_v, t_v, ws_v, wt_v, pj_v, codes_v, cot_v, len_ref,
    p3_v, gz_v, zc_v, mt_v, act_v, slope_v, g3_v, xt_v,
    halo_s, halo_r, ab_v,
    pw1, pw2, rc1, rc2,
    rel1, rel2, sum1, sum2, fin1, fin2,
    last1, last2, got1, got2, zs, rz,
    in_sem, halo_ss, halo_rs, a2a_ss, a2a_rs,
    core_ss, core_rs, x_ss, x_rs, y_ss, y_rs, z_ss, z_rs, g_ss, g_rs,
):
    tm = lax.axis_index("tm")
    clip = lax.axis_index("clip")
    z, y = tm // NY, tm % NY
    x, core = clip // NC, clip % NC

    def load(src, dst, i):
        copy = pltpu.make_async_copy(src, dst, in_sem.at[i])
        copy.start()
        return copy

    ld_pj = load(pj_hbm, pj_v, 0)
    ld_t0 = load(t_hbm.at[pl.ds(0, PAIR)], t_v.at[pl.ds(0, PAIR)], 1)
    ld_cd = load(codes_hbm, codes_v, 2)
    ld_ct = load(cot_hbm, cot_v, 3)
    ld_len = load(len_hbm, len_ref, 9)
    ld_t1 = load(t_hbm.at[pl.ds(PAIR, PAIR)], t_v.at[pl.ds(PAIR, PAIR)], 4)
    ld_wt = load(wt_hbm, wt_v, 5)
    ld_pre = load(pre_hbm, pre_v, 6)
    ld_x = load(x_hbm, x_v, 7)
    ld_ws = load(ws_hbm, ws_v, 8)

    barrier = pltpu.get_barrier_semaphore()

    @pl.loop(1, NT)
    def _(d):
        pl.semaphore_signal(
            barrier, inc=1, device_id=(lax.rem(tm + d, NT), clip), device_id_type=MESH
        )

    @pl.loop(1, NG)
    def _(d):
        pl.semaphore_signal(
            barrier, inc=1, device_id=(tm, lax.rem(clip + d, NG)), device_id_type=MESH
        )

    ld_pj.wait()
    row_l = iota((128, LAT), 0) % 32
    rep = ones_where(row_l == iota((128, LAT), 1))
    p3_v[...] = dot(rep, pj_v[...]).astype(BF16)

    rep_t = ones_where(iota((LAT, 128), 0) == iota((LAT, 128), 1) % 32)
    lane = iota((PAIR, 128), 1)
    lane_l = lane % 32
    row_id = iota((PAIR, 128), 0)
    spread = ones_where(iota((PAIR, 32), 0) // 16 == iota((PAIR, 32), 1))
    pick = ones_where(
        (iota((128, 128), 0) // 16 == (iota((128, 128), 1) % 32) // 6)
        & (iota((128, 128), 1) % 32 < LAT)
    )
    ld_len.wait()
    clip_len = len_ref[clip]

    def latents(fp):
        rows = pl.ds(fp * PAIR, PAIR)
        lat = dot_nt(t_v[rows, :], p3_v[...])
        cot = dot(cot_v[rows, :], rep_t)
        cd = codes_v[pl.ds(fp * 32, 32), :]
        packed = jnp.zeros((32, 128), F32)
        for piece in range(3):
            part = ((cd >> (6 * piece)) & 63).astype(F32).astype(BF16)
            place = ones_where(iota((16, 128), 1) == iota((16, 128), 0) + 16 * piece)
            packed = packed + dot(part, place)
        wide = dot(spread, packed.astype(BF16))
        own = jnp.where((lane < 48) & (lane % 16 == row_id % 16), wide, 0.0)
        six = dot(own.astype(BF16), pick).astype(I32)
        bit = (six >> (lane_l % 6)) & 1
        target = (2 * bit - 1).astype(F32)
        frame = tm * FR + fp * 2 + row_id // CELLS
        keep = (frame < clip_len) & (lane_l < LAT)
        grad = jnp.where(keep, cot + 0.5 * (lat - target), 0.0)
        gz_v[rows, :] = grad.astype(BF16)

    ld_t0.wait()
    ld_cd.wait()
    ld_ct.wait()
    latents(0)

    group = iota((CELLS, 128), 1) // 32

    def gz(f):
        return gz_v[f * CELLS : (f + 1) * CELLS, :].astype(F32)

    halo_s[...] = jnp.where(
        group == 0, 0.0, jnp.where(group == 2, gz(1), gz(0))
    ).astype(BF16)
    pl.semaphore_wait(barrier, NT - 1 + NG - 1)
    halo = pltpu.make_async_remote_copy(
        src_ref=halo_s, dst_ref=halo_r, send_sem=halo_ss, recv_sem=halo_rs,
        device_id=(lax.rem(tm + NT - 1, NT), clip), device_id_type=MESH,
    )
    halo.start()

    ld_t1.wait()
    latents(1)
    zc_v[0:CELLS, :] = jnp.where(
        group == 0, gz(0), jnp.where(group == 1, gz(1), jnp.where(group == 2, gz(2), 0.0))
    ).astype(BF16)
    zc_v[CELLS:PAIR, :] = jnp.where(
        group == 0, gz(1), jnp.where(group == 1, gz(2), jnp.where(group == 2, gz(3), 0.0))
    ).astype(BF16)

    ld_wt.wait()
    lane_g = iota((CMID, 128), 1) // 32
    fold = dot_nt(wt_v[2], p3_v[...])
    for k in range(2):
        fold = jnp.where(lane_g == k, dot_nt(wt_v[k], p3_v[...]), fold)
    mt_v[...] = fold.astype(BF16)

    ld_pre.wait()

    @pl.loop(0, ROWS // 64)
    def _(i):
        rows = pl.ds(pl.multiple_of(i * 64, 64), 64)
        v = pre_v[rows, :].astype(F32)
        s = 0.5 * jnp.tanh(0.5 * v) + 0.5
        a = v * s
        act_v[rows, :] = a.astype(BF16)
        slope_v[rows, :] = s + a * (1.0 - s)

    zero16 = jnp.zeros((16, CMID), BF16)

    def grad_pre(f):
        lo, hi = f * CELLS, (f + 1) * CELLS
        g = (dot_nt(zc_v[lo:hi, :], mt_v[...]) * slope_v[lo:hi, :]).astype(BF16)
        g3_v[1, lo:hi, :] = g
        g3_v[0, lo : hi - 16, :] = g[16:]
        g3_v[0, hi - 16 : hi, :] = zero16
        g3_v[2, lo + 16 : hi, :] = g[: CELLS - 16]
        g3_v[2, lo : lo + 16, :] = zero16

    row_p = iota((PAIR, CIN), 0) % 16

    def grad_x(fp):
        rows = slice(fp * PAIR, (fp + 1) * PAIR)
        back = []
        for b in range(3):
            acc = dot_nt(g3_v[0, rows, :], ws_v[b])
            for a in range(1, 3):
                acc = acc + dot_nt(g3_v[a, rows, :], ws_v[3 * a + b])
            back.append(acc)
        g = (
            back[1]
            + jnp.where(row_p != 15, pltpu.roll(back[0], PAIR - 1, 0), 0.0)
            + jnp.where(row_p != 0, pltpu.roll(back[2], 1, 0), 0.0)
        )
        for t in range(NT):
            both = jnp.concatenate(
                [g[8 * t : 8 * t + 8], g[CELLS + 8 * t : CELLS + 8 * t + 8]], axis=0
            )
            ab_v[t, fp] = both.astype(BF16)

        @pl.loop(1, NT)
        def _(d):
            to = lax.rem(tm + d, NT)
            pltpu.make_async_remote_copy(
                src_ref=ab_v.at[to, fp], dst_ref=out_hbm.at[2 * tm + fp],
                send_sem=a2a_ss, recv_sem=a2a_rs,
                device_id=(to, clip), device_id_type=MESH,
            ).start()

        pltpu.make_async_copy(ab_v.at[tm, fp], out_hbm.at[2 * tm + fp], a2a_rs).start()

    grad_pre(0)
    grad_pre(1)

    ld_x.wait()
    r = iota((CIN, CIN), 0)
    c = iota((CIN, CIN), 1)
    perm = ones_where(
        c == (r // 16) % 4 * 64 + (r // 8) % 2 * 32 + r // 64 * 8 + r % 8
    )
    shift_lo = ones_where((r == c - 1) & (c % 16 != 0))
    shift_hi = ones_where((r == c + 1) & (c % 16 != 15))
    for f in range(FR):
        lo, hi = f * CELLS, (f + 1) * CELLS
        xt = dot_nt(perm, x_v[lo:hi, :]).astype(BF16)
        xt_v[256:512, lo:hi] = xt
        xt_v[0:256, lo:hi] = dot(xt, shift_lo).astype(BF16)
        xt_v[512:768, lo:hi] = dot(xt, shift_hi).astype(BF16)

    halo.wait_recv()
    ahead = jnp.where(tm == NT - 1, 0.0, halo_r[...].astype(F32))
    zc_v[PAIR : PAIR + CELLS, :] = jnp.where(
        group == 0, gz(2), jnp.where(group == 1, gz(3), jnp.where(group == 3, ahead, 0.0))
    ).astype(BF16)
    zc_v[PAIR + CELLS :, :] = jnp.where(
        group == 0, gz(3), jnp.where(group == 3, 0.0, ahead)
    ).astype(BF16)
    grad_pre(2)
    grad_pre(3)

    def space(a, half):
        cols = pl.ds(pl.multiple_of(half * 256, 256), 256)
        acc = dot(xt_v[...], g3_v[a, :, cols])
        for b in range(3):
            for lb in range(2):
                block = acc[256 * b : 256 * b + 256, 128 * lb : 128 * lb + 128].astype(BF16)
                if a < 2:
                    i = 6 * a + 2 * b + lb
                    pw1[half, i // 3, i % 3] = block
                else:
                    for yy in range(NY):
                        pw2[half, 2 * b + lb, yy] = block[64 * yy : 64 * yy + 64]

    def factors():
        gt = dot_tn(zc_v[...], act_v[...])
        pt = dot_tn(gz_v[...], t_v[...])
        q_t = jnp.concatenate([gt[0:64], gt[64:96] + gt[96:128], pt[96:128]], axis=0)
        q = q_t.T
        for cc in range(NC):
            for yy in range(NY):
                for zp in range(NZ // 2):
                    lo = 16 * (2 * zp * NY + yy) + 8 * cc
                    hi = 16 * ((2 * zp + 1) * NY + yy) + 8 * cc
                    tile = jnp.concatenate([q[lo : lo + 8], q[hi : hi + 8]], axis=0).astype(BF16)
                    pw2[cc, 6, yy, 16 * zp : 16 * zp + 16, :] = tile
                    pw2[cc, 7, yy, 16 * zp : 16 * zp + 16, :] = tile

    other = 1 - core

    def core_copy(src, dst, i):
        return pltpu.make_async_remote_copy(
            src_ref=src, dst_ref=dst, send_sem=core_ss.at[i], recv_sem=core_rs.at[i],
            device_id=(tm, x * NC + other), device_id_type=MESH,
        )

    core_copies = (
        core_copy(pw1.at[other, pl.ds(0, 2)], rc1.at[pl.ds(0, 2)], 0),
        core_copy(pw1.at[other, pl.ds(2, 2)], rc1.at[pl.ds(2, 2)], 1),
        core_copy(pw2.at[other], rc2, 2),
    )
    space(0, other)
    core_copies[0].start()
    space(1, other)
    core_copies[1].start()
    factors()
    space(2, other)
    core_copies[2].start()
    for a in range(3):
        space(a, core)

    def x_copy(src, dst, to, i):
        return pltpu.make_async_remote_copy(
            src_ref=src, dst_ref=dst, send_sem=x_ss.at[i], recv_sem=x_rs.at[i],
            device_id=(tm, to * NC + core), device_id_type=MESH,
        )

    def y_copy(src, dst, to, i):
        return pltpu.make_async_remote_copy(
            src_ref=src, dst_ref=dst, send_sem=y_ss.at[i], recv_sem=y_rs.at[i],
            device_id=(z * NY + to, clip), device_id_type=MESH,
        )

    def plus(a, b):
        return (a.astype(F32) + b.astype(F32)).astype(BF16)

    def halves1(ref, *at):
        return [ref.at[(*at, slice(None), pl.ds(128 * h, 128))] for h in range(2)]

    def halves2(ref, *at):
        return [ref.at[(*at, pl.ds(4 * h, 4))] for h in range(2)]

    def add1(chunk):
        for s in range(3):
            sum1[chunk, s] = plus(pw1[core, chunk, s], rc1[chunk, s])

    def add2(chunk):
        for s in range(8):
            sum2[chunk, s] = plus(pw2[core, s, chunk], rc2[s, chunk])

    def first(me, copy, halves, add, rel, sm, fin):
        left, right, far = lax.rem(me + 3, 4), lax.rem(me + 1, 4), lax.rem(me + 2, 4)
        add(far)
        a, b = halves(sm, far)
        copies = [copy(a, rel.at[0], left, 0), copy(b, rel.at[1], right, 1)]
        copies[0].start()
        copies[1].start()
        add(left)
        copies.append(copy(halves(sm, left)[1], halves(fin, 1)[1], left, 2))
        copies[2].start()
        add(right)
        copies.append(copy(halves(sm, right)[0], halves(fin, 0)[0], right, 3))
        copies[3].start()
        add(me)
        return copies

    def second(me, copy, halves, relay, sm, fin, copies):
        left, right = lax.rem(me + 3, 4), lax.rem(me + 1, 4)
        copies[0].wait_recv()
        relay(left, 0)
        copies.append(copy(halves(sm, left)[0], halves(fin, 1)[0], left, 4))
        copies[4].start()
        copies[1].wait_recv()
        relay(right, 1)
        copies.append(copy(halves(sm, right)[1], halves(fin, 0)[1], right, 5))
        copies[5].start()

    def relay1(chunk, h):
        for s in range(3):
            rows = slice(128 * h, 128 * h + 128)
            sum1[chunk, s, rows] = plus(sum1[chunk, s, rows], rel1[h, s])

    def relay2(chunk, h):
        for s in range(4):
            sum2[chunk, 4 * h + s] = plus(sum2[chunk, 4 * h + s], rel2[h, s])

    core_copies[0].wait_recv()
    core_copies[1].wait_recv()
    copies1 = first(x, x_copy, halves1, add1, rel1, sum1, fin1)
    core_copies[2].wait_recv()
    copies2 = first(y, y_copy, halves2, add2, rel2, sum2, fin2)

    ld_ws.wait()
    grad_x(0)

    second(y, y_copy, halves2, relay2, sum2, fin2, copies2)
    second(x, x_copy, halves1, relay1, sum1, fin1, copies1)

    grad_x(1)

    for copy in copies2[2:]:
        copy.wait_recv()
    for s in range(8):
        last2[s] = (
            sum2[y, s].astype(F32) + fin2[0, s].astype(F32) + fin2[1, s].astype(F32)
        ).astype(BF16)
    for d in range(1, NX):
        to = lax.rem(x + d, NX)
        copy = x_copy(last2.at[pl.ds(2 * to, 2)], got2.at[d - 1], to, 5 + d)
        copy.start()
        copies2.append(copy)
    for copy in copies1[2:]:
        copy.wait_recv()
    for s in range(3):
        tot = sum1[x, s].astype(F32) + fin1[0, s].astype(F32) + fin1[1, s].astype(F32)
        tot = tot.astype(BF16)
        for yy in range(NY):
            last1[yy, s] = tot[64 * yy : 64 * yy + 64]
    for d in range(1, NY):
        to = lax.rem(y + d, NY)
        copy = y_copy(last1.at[to], got1.at[d - 1], to, 5 + d)
        copy.start()
        copies1.append(copy)
    for copy in copies2[6:] + copies1[6:]:
        copy.wait_recv()
    tots = []
    for s in range(5):
        tot = (last1[y, s] if s < 3 else last2[2 * x + s - 3]).astype(F32)
        for d in range(3):
            tot = tot + (got1[d, s] if s < 3 else got2[d, s - 3]).astype(F32)
        tots.append(tot)
    blank = jnp.zeros((8, 128), F32)
    for zz in range(NZ):
        eights = [tot[8 * zz : 8 * zz + 8] for tot in tots] + [blank]
        for i in range(3):
            zs[zz, 16 * i : 16 * i + 16] = jnp.concatenate(
                eights[2 * i : 2 * i + 2], axis=0
            ).astype(BF16)

    z_copies = []
    for d in range(1, NZ):
        to = lax.rem(z + d, NZ)
        copy = pltpu.make_async_remote_copy(
            src_ref=zs.at[to], dst_ref=rz.at[d - 1],
            send_sem=z_ss.at[d - 1], recv_sem=z_rs.at[d - 1],
            device_id=(to * NY + y, clip), device_id_type=MESH,
        )
        copy.start()
        z_copies.append(copy)
    for copy in z_copies:
        copy.wait_recv()
    tot = zs[z].astype(F32)
    for d in range(NZ - 1):
        tot = tot + rz[d].astype(F32)
    ra[core, x] = (tot * SCALE).astype(BF16)

    g_copies = []
    for d in range(1, NX):
        copy = pltpu.make_async_remote_copy(
            src_ref=ra.at[core, x], dst_ref=ra.at[core, x],
            send_sem=g_ss.at[d - 1], recv_sem=g_rs.at[d - 1],
            device_id=(tm, lax.rem(x + d, NX) * NC + core), device_id_type=MESH,
        )
        copy.start()
        g_copies.append(copy)
    for copy in g_copies:
        copy.wait_recv()
    copy = pltpu.make_async_remote_copy(
        src_ref=ra.at[core], dst_ref=ra.at[core],
        send_sem=g_ss.at[NX - 1], recv_sem=g_rs.at[NX - 1],
        device_id=(tm, x * NC + other), device_id_type=MESH,
    )
    copy.start()
    g_copies.append(copy)
    copy.wait_recv()

    halo.wait_send()
    for copy in [*core_copies, *copies1, *copies2, *z_copies, *g_copies]:
        copy.wait_send()
    sent = ab_v.at[pl.ds(0, NT - 1)]
    pltpu.make_async_copy(sent, sent, a2a_ss).wait()
    pltpu.make_async_copy(out_hbm, out_hbm, a2a_rs).wait()


def finish(raw, ra, pj_ref, out_hbm, space_ref, time_ref, proj_ref, sem):
    whole = pltpu.make_async_copy(raw, out_hbm, sem)
    whole.start()
    for cc in range(NC):
        for i in range(18):
            a, b, lb = i // 6, i // 2 % 3, i % 2
            if a < 2:
                xx, s = i // 3, i % 3
            else:
                xx, s = (i - 12) // 2, 3 + i % 2
            tile = ra[cc, xx, 16 * (s // 2) : 16 * (s // 2) + 16].astype(F32)
            lo = 256 * cc + 128 * lb
            space_ref[3 * a + b, :, lo : lo + 128] = tile[8 * (s % 2) : 8 * (s % 2) + 8]
    qs = jnp.concatenate([ra[cc, 3, 16:32].astype(F32)[8:16] for cc in range(NC)], axis=0)
    qs = qs.astype(BF16)
    for k in range(3):
        take = ones_where(iota((128, LAT), 0) == iota((128, LAT), 1) + 32 * k)
        time_ref[k] = dot(dot(qs, take).astype(BF16), pj_ref[...])
    take = ones_where(iota((128, LAT), 0) == iota((128, LAT), 1) + 96)
    proj_ref[...] = dot(qs, take)
    whole.wait()


def per_device(block_input, pre_act, time_out, w_space, w_time, proj, codes, cotan, lengths):
    args = (
        block_input.reshape(ROWS, CIN),
        pre_act.reshape(ROWS, CMID),
        time_out.reshape(ROWS, CMID),
        w_space.transpose(1, 2, 0, 3).reshape(9, CIN, CMID),
        w_time.transpose(1, 0, 2),
        proj.T,
        codes.reshape(FR * 16, 16),
        cotan.reshape(ROWS, LAT),
        lengths,
    )
    hbm = pl.BlockSpec(memory_space=pltpu.HBM)
    held = [pltpu.with_memory_space_constraint(a, pltpu.HBM) for a in args]
    vmem = pl.BlockSpec(memory_space=pltpu.VMEM)
    dma = pltpu.SemaphoreType.DMA
    v = pltpu.VMEM
    limit = 40 * 1024 * 1024
    raw, sums = pl.pallas_call(
        kernel,
        out_shape=(pltpu.VMEM((2 * NT, 16, CIN), BF16), pltpu.VMEM((NC, NX, 48, 128), BF16)),
        in_specs=[hbm] * 9,
        out_specs=(vmem, vmem),
        scratch_shapes=[
            v((ROWS, CIN), BF16), v((ROWS, CMID), BF16), v((ROWS, CMID), BF16),
            v((9, CIN, CMID), BF16), v((3, CMID, CMID), BF16), v((LAT, CMID), BF16),
            v((FR * 16, 16), I32), v((ROWS, LAT), BF16), pltpu.SMEM((NG,), I32),
            v((128, CMID), BF16), v((ROWS, 128), BF16), v((ROWS, 128), BF16),
            v((CMID, 128), BF16), v((ROWS, CMID), BF16), v((ROWS, CMID), F32),
            v((3, ROWS, CMID), BF16), v((768, ROWS), BF16),
            v((CELLS, 128), BF16), v((CELLS, 128), BF16), v((NT, 2, 16, CIN), BF16),
            v((NC, NX, 3, 256, 128), BF16), v((NC, 8, NY, 64, 128), BF16),
            v((NX, 3, 256, 128), BF16), v((8, NY, 64, 128), BF16),
            v((2, 3, 128, 128), BF16), v((2, 4, 64, 128), BF16),
            v((NX, 3, 256, 128), BF16), v((NY, 8, 64, 128), BF16),
            v((2, 3, 256, 128), BF16), v((2, 8, 64, 128), BF16),
            v((NY, 3, 64, 128), BF16), v((8, 64, 128), BF16),
            v((NY - 1, 3, 64, 128), BF16), v((NX - 1, 2, 64, 128), BF16),
            v((NZ, 48, 128), BF16), v((NZ - 1, 48, 128), BF16),
            dma((10,)), dma(()), dma(()), dma(()), dma(()),
            dma((3,)), dma((3,)), dma((9,)), dma((9,)), dma((9,)), dma((9,)),
            dma((NZ - 1,)), dma((NZ - 1,)), dma((NX,)), dma((NX,)),
        ],
        compiler_params=pltpu.CompilerParams(
            collective_id=0, has_side_effects=True, vmem_limit_bytes=limit
        ),
    )(*held)
    out, space, time, projg = pl.pallas_call(
        finish,
        out_shape=(
            jax.ShapeDtypeStruct((2 * NT, 16, CIN), BF16),
            jax.ShapeDtypeStruct((9, 8, CMID), F32),
            jax.ShapeDtypeStruct((3, 16, CMID), F32),
            jax.ShapeDtypeStruct((16, LAT), F32),
        ),
        in_specs=[vmem, vmem, vmem],
        out_specs=(hbm, vmem, vmem, vmem),
        scratch_shapes=[dma(())],
        compiler_params=pltpu.CompilerParams(vmem_limit_bytes=8 * 1024 * 1024),
    )(raw, sums, args[5])
    return (
        out.reshape(1, FR * NT, 8, CIN),
        space.reshape(3, 3, 8, CMID).transpose(2, 0, 1, 3),
        time.transpose(1, 0, 2),
        projg,
    )


def solution(mesh):
    placed = (
        P("clip", "tm", None, None, None),
        P("clip", "tm", None, None, None),
        P("clip", "tm", None, None, None),
        P(),
        P(),
        P(),
        P("clip", "tm", None, None),
        P("clip", "tm", None, None, None),
        P(),
    )
    return jax.shard_map(
        per_device,
        mesh=mesh,
        in_specs=placed,
        out_specs=(
            P("clip", None, "tm", None),
            P("tm", None, None, None),
            P("tm", None, None),
            P("tm", None),
        ),
        check_vma=False,
    )
```

```python
import jax
import jax.numpy as jnp
from jax import lax
from jax.experimental import pallas as pl
from jax.experimental.pallas import tpu as pltpu
from jax.sharding import PartitionSpec as P

MESH = pl.DeviceIdType.MESH
F32 = jnp.float32
BF16 = jnp.bfloat16
I32 = jnp.int32

NZ, NY, NX, NC = 8, 4, 4, 2
NT, NG = NZ * NY, NX * NC
FR, CELLS, CIN, CMID, LAT = 4, 256, 256, 512, 18
ROWS = FR * CELLS
PAIR = 2 * CELLS
SCALE = 1.0 / 512.0

NT_DIMS = (((1,), (1,)), ((), ()))
TN_DIMS = (((0,), (0,)), ((), ()))


def iota(shape, dim):
    return lax.broadcasted_iota(I32, shape, dim)


def ones_where(cond):
    return jnp.where(cond, 1.0, 0.0).astype(BF16)


def dot(a, b):
    return jnp.dot(a, b, preferred_element_type=F32)


def dot_nt(a, b):
    return lax.dot_general(a, b, NT_DIMS, preferred_element_type=F32)


def dot_tn(a, b):
    return lax.dot_general(a, b, TN_DIMS, preferred_element_type=F32)


def kernel(
    x_hbm, pre_hbm, t_hbm, ws_hbm, wt_hbm, pj_hbm, codes_hbm, cot_hbm, len_hbm,
    out_hbm, ra,
    x_v, pre_v, t_v, ws_v, wt_v, pj_v, codes_v, cot_v, len_ref,
    p3_v, gz_v, zc_v, mt_v, act_v, slope_v, g3_v, xt_v,
    halo_s, halo_r, ab_v,
    pw1, pw2, rc1, rc2,
    rel1, rel2, sum1, sum2, fin1, fin2,
    last1, last2, got1, got2, zs, rz,
    in_sem, halo_ss, halo_rs, a2a_ss, a2a_rs,
    core_ss, core_rs, x_ss, x_rs, y_ss, y_rs, z_ss, z_rs, g_ss, g_rs,
):
    tm = lax.axis_index("tm")
    clip = lax.axis_index("clip")
    z, y = tm // NY, tm % NY
    x, core = clip // NC, clip % NC

    def load(src, dst, i):
        copy = pltpu.make_async_copy(src, dst, in_sem.at[i])
        copy.start()
        return copy

    ld_pj = load(pj_hbm, pj_v, 0)
    ld_t0 = load(t_hbm.at[pl.ds(0, PAIR)], t_v.at[pl.ds(0, PAIR)], 1)
    ld_cd = load(codes_hbm, codes_v, 2)
    ld_ct = load(cot_hbm, cot_v, 3)
    ld_len = load(len_hbm, len_ref, 9)
    ld_t1 = load(t_hbm.at[pl.ds(PAIR, PAIR)], t_v.at[pl.ds(PAIR, PAIR)], 4)
    ld_wt = load(wt_hbm, wt_v, 5)
    ld_pre = load(pre_hbm, pre_v, 6)
    ld_x = load(x_hbm, x_v, 7)
    ld_ws = load(ws_hbm, ws_v, 8)

    barrier = pltpu.get_barrier_semaphore()

    @pl.loop(1, NT)
    def _(d):
        pl.semaphore_signal(
            barrier, inc=1, device_id=(lax.rem(tm + d, NT), clip), device_id_type=MESH
        )

    @pl.loop(1, NG)
    def _(d):
        pl.semaphore_signal(
            barrier, inc=1, device_id=(tm, lax.rem(clip + d, NG)), device_id_type=MESH
        )

    ld_pj.wait()
    row_l = iota((128, LAT), 0) % 32
    rep = ones_where(row_l == iota((128, LAT), 1))
    p3_v[...] = dot(rep, pj_v[...]).astype(BF16)

    rep_t = ones_where(iota((LAT, 128), 0) == iota((LAT, 128), 1) % 32)
    lane = iota((PAIR, 128), 1)
    lane_l = lane % 32
    row_id = iota((PAIR, 128), 0)
    spread = ones_where(iota((PAIR, 32), 0) // 16 == iota((PAIR, 32), 1))
    pick = ones_where(
        (iota((128, 128), 0) // 16 == (iota((128, 128), 1) % 32) // 6)
        & (iota((128, 128), 1) % 32 < LAT)
    )
    ld_len.wait()
    clip_len = len_ref[clip]

    def latents(fp):
        rows = pl.ds(fp * PAIR, PAIR)
        lat = dot_nt(t_v[rows, :], p3_v[...])
        cot = dot(cot_v[rows, :], rep_t)
        cd = codes_v[pl.ds(fp * 32, 32), :]
        packed = jnp.zeros((32, 128), F32)
        for piece in range(3):
            part = ((cd >> (6 * piece)) & 63).astype(F32).astype(BF16)
            place = ones_where(iota((16, 128), 1) == iota((16, 128), 0) + 16 * piece)
            packed = packed + dot(part, place)
        wide = dot(spread, packed.astype(BF16))
        own = jnp.where((lane < 48) & (lane % 16 == row_id % 16), wide, 0.0)
        six = dot(own.astype(BF16), pick).astype(I32)
        bit = (six >> (lane_l % 6)) & 1
        target = (2 * bit - 1).astype(F32)
        frame = tm * FR + fp * 2 + row_id // CELLS
        keep = (frame < clip_len) & (lane_l < LAT)
        grad = jnp.where(keep, cot + 0.5 * (lat - target), 0.0)
        gz_v[rows, :] = grad.astype(BF16)

    ld_t0.wait()
    ld_cd.wait()
    ld_ct.wait()
    latents(0)

    group = iota((CELLS, 128), 1) // 32

    def gz(f):
        return gz_v[f * CELLS : (f + 1) * CELLS, :].astype(F32)

    halo_s[...] = jnp.where(
        group == 0, 0.0, jnp.where(group == 2, gz(1), gz(0))
    ).astype(BF16)
    pl.semaphore_wait(barrier, NT - 1 + NG - 1)
    halo = pltpu.make_async_remote_copy(
        src_ref=halo_s, dst_ref=halo_r, send_sem=halo_ss, recv_sem=halo_rs,
        device_id=(lax.rem(tm + NT - 1, NT), clip), device_id_type=MESH,
    )
    halo.start()

    ld_t1.wait()
    latents(1)
    zc_v[0:CELLS, :] = jnp.where(
        group == 0, gz(0), jnp.where(group == 1, gz(1), jnp.where(group == 2, gz(2), 0.0))
    ).astype(BF16)
    zc_v[CELLS:PAIR, :] = jnp.where(
        group == 0, gz(1), jnp.where(group == 1, gz(2), jnp.where(group == 2, gz(3), 0.0))
    ).astype(BF16)

    ld_wt.wait()
    lane_g = iota((CMID, 128), 1) // 32
    fold = dot_nt(wt_v[2], p3_v[...])
    for k in range(2):
        fold = jnp.where(lane_g == k, dot_nt(wt_v[k], p3_v[...]), fold)
    mt_v[...] = fold.astype(BF16)

    ld_pre.wait()

    @pl.loop(0, ROWS // 64)
    def _(i):
        rows = pl.ds(pl.multiple_of(i * 64, 64), 64)
        v = pre_v[rows, :].astype(F32)
        s = 0.5 * jnp.tanh(0.5 * v) + 0.5
        a = v * s
        act_v[rows, :] = a.astype(BF16)
        slope_v[rows, :] = s + a * (1.0 - s)

    zero16 = jnp.zeros((16, CMID), BF16)

    def grad_pre(f):
        lo, hi = f * CELLS, (f + 1) * CELLS
        g = (dot_nt(zc_v[lo:hi, :], mt_v[...]) * slope_v[lo:hi, :]).astype(BF16)
        g3_v[1, lo:hi, :] = g
        g3_v[0, lo : hi - 16, :] = g[16:]
        g3_v[0, hi - 16 : hi, :] = zero16
        g3_v[2, lo + 16 : hi, :] = g[: CELLS - 16]
        g3_v[2, lo : lo + 16, :] = zero16

    row_p = iota((PAIR, CIN), 0) % 16

    def grad_x(fp):
        rows = slice(fp * PAIR, (fp + 1) * PAIR)
        back = []
        for b in range(3):
            acc = dot_nt(g3_v[0, rows, :], ws_v[b])
            for a in range(1, 3):
                acc = acc + dot_nt(g3_v[a, rows, :], ws_v[3 * a + b])
            back.append(acc)
        g = (
            back[1]
            + jnp.where(row_p != 15, pltpu.roll(back[0], PAIR - 1, 0), 0.0)
            + jnp.where(row_p != 0, pltpu.roll(back[2], 1, 0), 0.0)
        )
        for t in range(NT):
            both = jnp.concatenate(
                [g[8 * t : 8 * t + 8], g[CELLS + 8 * t : CELLS + 8 * t + 8]], axis=0
            )
            ab_v[t, fp] = both.astype(BF16)

    def send_x(fp):
        @pl.loop(1, NT)
        def _(d):
            to = lax.rem(z + d % NZ, NZ) * NY + lax.rem(y + d // NZ, NY)
            pltpu.make_async_remote_copy(
                src_ref=ab_v.at[to, fp], dst_ref=out_hbm.at[2 * tm + fp],
                send_sem=a2a_ss, recv_sem=a2a_rs,
                device_id=(to, clip), device_id_type=MESH,
            ).start()

        pltpu.make_async_copy(ab_v.at[tm, fp], out_hbm.at[2 * tm + fp], a2a_rs).start()

    grad_pre(0)
    grad_pre(1)

    ld_x.wait()
    r = iota((CIN, CIN), 0)
    c = iota((CIN, CIN), 1)
    perm = ones_where(
        c == (r // 16) % 4 * 64 + (r // 8) % 2 * 32 + r // 64 * 8 + r % 8
    )
    shift_lo = ones_where((r == c - 1) & (c % 16 != 0))
    shift_hi = ones_where((r == c + 1) & (c % 16 != 15))
    for f in range(FR):
        lo, hi = f * CELLS, (f + 1) * CELLS
        xt = dot_nt(perm, x_v[lo:hi, :]).astype(BF16)
        xt_v[256:512, lo:hi] = xt
        xt_v[0:256, lo:hi] = dot(xt, shift_lo).astype(BF16)
        xt_v[512:768, lo:hi] = dot(xt, shift_hi).astype(BF16)

    halo.wait_recv()
    ahead = jnp.where(tm == NT - 1, 0.0, halo_r[...].astype(F32))
    zc_v[PAIR : PAIR + CELLS, :] = jnp.where(
        group == 0, gz(2), jnp.where(group == 1, gz(3), jnp.where(group == 3, ahead, 0.0))
    ).astype(BF16)
    zc_v[PAIR + CELLS :, :] = jnp.where(
        group == 0, gz(3), jnp.where(group == 3, 0.0, ahead)
    ).astype(BF16)
    grad_pre(2)
    grad_pre(3)

    def space(a, half):
        cols = pl.ds(pl.multiple_of(half * 256, 256), 256)
        acc = dot(xt_v[...], g3_v[a, :, cols])
        for b in range(3):
            for lb in range(2):
                block = acc[256 * b : 256 * b + 256, 128 * lb : 128 * lb + 128].astype(BF16)
                if a < 2:
                    i = 6 * a + 2 * b + lb
                    pw1[half, i // 3, i % 3] = block
                else:
                    for yy in range(NY):
                        pw2[half, 2 * b + lb, yy] = block[64 * yy : 64 * yy + 64]

    def factors():
        gt = dot_tn(zc_v[...], act_v[...])
        pt = dot_tn(gz_v[...], t_v[...])
        q_t = jnp.concatenate([gt[0:64], gt[64:96] + gt[96:128], pt[96:128]], axis=0)
        q = q_t.T
        for cc in range(NC):
            for yy in range(NY):
                for zp in range(NZ // 2):
                    lo = 16 * (2 * zp * NY + yy) + 8 * cc
                    hi = 16 * ((2 * zp + 1) * NY + yy) + 8 * cc
                    tile = jnp.concatenate([q[lo : lo + 8], q[hi : hi + 8]], axis=0).astype(BF16)
                    pw2[cc, 6, yy, 16 * zp : 16 * zp + 16, :] = tile
                    pw2[cc, 7, yy, 16 * zp : 16 * zp + 16, :] = tile

    other = 1 - core

    def core_copy(src, dst, i):
        return pltpu.make_async_remote_copy(
            src_ref=src, dst_ref=dst, send_sem=core_ss.at[i], recv_sem=core_rs.at[i],
            device_id=(tm, x * NC + other), device_id_type=MESH,
        )

    core_copies = (
        core_copy(pw1.at[other, pl.ds(0, 2)], rc1.at[pl.ds(0, 2)], 0),
        core_copy(pw1.at[other, pl.ds(2, 2)], rc1.at[pl.ds(2, 2)], 1),
        core_copy(pw2.at[other], rc2, 2),
    )
    space(0, other)
    core_copies[0].start()
    space(1, other)
    core_copies[1].start()
    factors()
    space(2, other)
    core_copies[2].start()
    for a in range(3):
        space(a, core)

    def x_copy(src, dst, to, i):
        return pltpu.make_async_remote_copy(
            src_ref=src, dst_ref=dst, send_sem=x_ss.at[i], recv_sem=x_rs.at[i],
            device_id=(tm, to * NC + core), device_id_type=MESH,
        )

    def y_copy(src, dst, to, i):
        return pltpu.make_async_remote_copy(
            src_ref=src, dst_ref=dst, send_sem=y_ss.at[i], recv_sem=y_rs.at[i],
            device_id=(z * NY + to, clip), device_id_type=MESH,
        )

    def plus(a, b):
        return (a.astype(F32) + b.astype(F32)).astype(BF16)

    def halves1(ref, *at):
        return [ref.at[(*at, slice(None), pl.ds(128 * h, 128))] for h in range(2)]

    def halves2(ref, *at):
        return [ref.at[(*at, pl.ds(4 * h, 4))] for h in range(2)]

    def add1(chunk):
        for s in range(3):
            sum1[chunk, s] = plus(pw1[core, chunk, s], rc1[chunk, s])

    def add2(chunk):
        for s in range(8):
            sum2[chunk, s] = plus(pw2[core, s, chunk], rc2[s, chunk])

    def first(me, copy, halves, add, rel, sm, fin):
        left, right, far = lax.rem(me + 3, 4), lax.rem(me + 1, 4), lax.rem(me + 2, 4)
        add(far)
        a, b = halves(sm, far)
        copies = [copy(a, rel.at[0], left, 0), copy(b, rel.at[1], right, 1)]
        copies[0].start()
        copies[1].start()
        add(left)
        copies.append(copy(halves(sm, left)[1], halves(fin, 1)[1], left, 2))
        copies[2].start()
        add(right)
        copies.append(copy(halves(sm, right)[0], halves(fin, 0)[0], right, 3))
        copies[3].start()
        add(me)
        return copies

    def second(me, copy, halves, relay, sm, fin, copies):
        left, right = lax.rem(me + 3, 4), lax.rem(me + 1, 4)
        copies[0].wait_recv()
        relay(left, 0)
        copies.append(copy(halves(sm, left)[0], halves(fin, 1)[0], left, 4))
        copies[4].start()
        copies[1].wait_recv()
        relay(right, 1)
        copies.append(copy(halves(sm, right)[1], halves(fin, 0)[1], right, 5))
        copies[5].start()

    def relay1(chunk, h):
        for s in range(3):
            rows = slice(128 * h, 128 * h + 128)
            sum1[chunk, s, rows] = plus(sum1[chunk, s, rows], rel1[h, s])

    def relay2(chunk, h):
        for s in range(4):
            sum2[chunk, 4 * h + s] = plus(sum2[chunk, 4 * h + s], rel2[h, s])

    core_copies[0].wait_recv()
    core_copies[1].wait_recv()
    copies1 = first(x, x_copy, halves1, add1, rel1, sum1, fin1)
    core_copies[2].wait_recv()
    copies2 = first(y, y_copy, halves2, add2, rel2, sum2, fin2)

    ld_ws.wait()
    grad_x(0)
    send_x(0)

    second(y, y_copy, halves2, relay2, sum2, fin2, copies2)
    second(x, x_copy, halves1, relay1, sum1, fin1, copies1)

    grad_x(1)
    send_x(1)

    for copy in copies2[2:]:
        copy.wait_recv()
    for s in range(8):
        last2[s] = (
            sum2[y, s].astype(F32) + fin2[0, s].astype(F32) + fin2[1, s].astype(F32)
        ).astype(BF16)
    for d in range(1, NX):
        to = lax.rem(x + d, NX)
        copy = x_copy(last2.at[pl.ds(2 * to, 2)], got2.at[d - 1], to, 5 + d)
        copy.start()
        copies2.append(copy)
    for copy in copies1[2:]:
        copy.wait_recv()
    for s in range(3):
        tot = sum1[x, s].astype(F32) + fin1[0, s].astype(F32) + fin1[1, s].astype(F32)
        tot = tot.astype(BF16)
        for yy in range(NY):
            last1[yy, s] = tot[64 * yy : 64 * yy + 64]
    for d in range(1, NY):
        to = lax.rem(y + d, NY)
        copy = y_copy(last1.at[to], got1.at[d - 1], to, 5 + d)
        copy.start()
        copies1.append(copy)
    for copy in copies2[6:] + copies1[6:]:
        copy.wait_recv()
    tots = []
    for s in range(5):
        tot = (last1[y, s] if s < 3 else last2[2 * x + s - 3]).astype(F32)
        for d in range(3):
            tot = tot + (got1[d, s] if s < 3 else got2[d, s - 3]).astype(F32)
        tots.append(tot)
    blank = jnp.zeros((8, 128), F32)
    for zz in range(NZ):
        eights = [tot[8 * zz : 8 * zz + 8] for tot in tots] + [blank]
        for i in range(3):
            zs[zz, 16 * i : 16 * i + 16] = jnp.concatenate(
                eights[2 * i : 2 * i + 2], axis=0
            ).astype(BF16)

    z_copies = []
    for d in range(1, NZ):
        to = lax.rem(z + d, NZ)
        copy = pltpu.make_async_remote_copy(
            src_ref=zs.at[to], dst_ref=rz.at[d - 1],
            send_sem=z_ss.at[d - 1], recv_sem=z_rs.at[d - 1],
            device_id=(to * NY + y, clip), device_id_type=MESH,
        )
        copy.start()
        z_copies.append(copy)
    for copy in z_copies:
        copy.wait_recv()
    tot = zs[z].astype(F32)
    for d in range(NZ - 1):
        tot = tot + rz[d].astype(F32)
    ra[core, x] = (tot * SCALE).astype(BF16)

    g_copies = []
    for d in range(1, NX):
        copy = pltpu.make_async_remote_copy(
            src_ref=ra.at[core, x], dst_ref=ra.at[core, x],
            send_sem=g_ss.at[d - 1], recv_sem=g_rs.at[d - 1],
            device_id=(tm, lax.rem(x + d, NX) * NC + core), device_id_type=MESH,
        )
        copy.start()
        g_copies.append(copy)
    for copy in g_copies:
        copy.wait_recv()
    copy = pltpu.make_async_remote_copy(
        src_ref=ra.at[core], dst_ref=ra.at[core],
        send_sem=g_ss.at[NX - 1], recv_sem=g_rs.at[NX - 1],
        device_id=(tm, x * NC + other), device_id_type=MESH,
    )
    copy.start()
    g_copies.append(copy)
    copy.wait_recv()

    halo.wait_send()
    for copy in [*core_copies, *copies1, *copies2, *z_copies, *g_copies]:
        copy.wait_send()
    sent = ab_v.at[pl.ds(0, NT - 1)]
    pltpu.make_async_copy(sent, sent, a2a_ss).wait()
    pltpu.make_async_copy(out_hbm, out_hbm, a2a_rs).wait()


def finish(raw, ra, pj_ref, out_hbm, space_ref, time_ref, proj_ref, sem):
    whole = pltpu.make_async_copy(raw, out_hbm, sem)
    whole.start()
    for cc in range(NC):
        for i in range(18):
            a, b, lb = i // 6, i // 2 % 3, i % 2
            if a < 2:
                xx, s = i // 3, i % 3
            else:
                xx, s = (i - 12) // 2, 3 + i % 2
            tile = ra[cc, xx, 16 * (s // 2) : 16 * (s // 2) + 16].astype(F32)
            lo = 256 * cc + 128 * lb
            space_ref[3 * a + b, :, lo : lo + 128] = tile[8 * (s % 2) : 8 * (s % 2) + 8]
    qs = jnp.concatenate([ra[cc, 3, 16:32].astype(F32)[8:16] for cc in range(NC)], axis=0)
    qs = qs.astype(BF16)
    for k in range(3):
        take = ones_where(iota((128, LAT), 0) == iota((128, LAT), 1) + 32 * k)
        time_ref[k] = dot(dot(qs, take).astype(BF16), pj_ref[...])
    take = ones_where(iota((128, LAT), 0) == iota((128, LAT), 1) + 96)
    proj_ref[...] = dot(qs, take)
    whole.wait()


def per_device(block_input, pre_act, time_out, w_space, w_time, proj, codes, cotan, lengths):
    args = (
        block_input.reshape(ROWS, CIN),
        pre_act.reshape(ROWS, CMID),
        time_out.reshape(ROWS, CMID),
        w_space.transpose(1, 2, 0, 3).reshape(9, CIN, CMID),
        w_time.transpose(1, 0, 2),
        proj.T,
        codes.reshape(FR * 16, 16),
        cotan.reshape(ROWS, LAT),
        lengths,
    )
    hbm = pl.BlockSpec(memory_space=pltpu.HBM)
    held = [pltpu.with_memory_space_constraint(a, pltpu.HBM) for a in args]
    vmem = pl.BlockSpec(memory_space=pltpu.VMEM)
    dma = pltpu.SemaphoreType.DMA
    v = pltpu.VMEM
    limit = 40 * 1024 * 1024
    raw, sums = pl.pallas_call(
        kernel,
        out_shape=(pltpu.VMEM((2 * NT, 16, CIN), BF16), pltpu.VMEM((NC, NX, 48, 128), BF16)),
        in_specs=[hbm] * 9,
        out_specs=(vmem, vmem),
        scratch_shapes=[
            v((ROWS, CIN), BF16), v((ROWS, CMID), BF16), v((ROWS, CMID), BF16),
            v((9, CIN, CMID), BF16), v((3, CMID, CMID), BF16), v((LAT, CMID), BF16),
            v((FR * 16, 16), I32), v((ROWS, LAT), BF16), pltpu.SMEM((NG,), I32),
            v((128, CMID), BF16), v((ROWS, 128), BF16), v((ROWS, 128), BF16),
            v((CMID, 128), BF16), v((ROWS, CMID), BF16), v((ROWS, CMID), F32),
            v((3, ROWS, CMID), BF16), v((768, ROWS), BF16),
            v((CELLS, 128), BF16), v((CELLS, 128), BF16), v((NT, 2, 16, CIN), BF16),
            v((NC, NX, 3, 256, 128), BF16), v((NC, 8, NY, 64, 128), BF16),
            v((NX, 3, 256, 128), BF16), v((8, NY, 64, 128), BF16),
            v((2, 3, 128, 128), BF16), v((2, 4, 64, 128), BF16),
            v((NX, 3, 256, 128), BF16), v((NY, 8, 64, 128), BF16),
            v((2, 3, 256, 128), BF16), v((2, 8, 64, 128), BF16),
            v((NY, 3, 64, 128), BF16), v((8, 64, 128), BF16),
            v((NY - 1, 3, 64, 128), BF16), v((NX - 1, 2, 64, 128), BF16),
            v((NZ, 48, 128), BF16), v((NZ - 1, 48, 128), BF16),
            dma((10,)), dma(()), dma(()), dma(()), dma(()),
            dma((3,)), dma((3,)), dma((9,)), dma((9,)), dma((9,)), dma((9,)),
            dma((NZ - 1,)), dma((NZ - 1,)), dma((NX,)), dma((NX,)),
        ],
        compiler_params=pltpu.CompilerParams(
            collective_id=0, has_side_effects=True, vmem_limit_bytes=limit
        ),
    )(*held)
    out, space, time, projg = pl.pallas_call(
        finish,
        out_shape=(
            jax.ShapeDtypeStruct((2 * NT, 16, CIN), BF16),
            jax.ShapeDtypeStruct((9, 8, CMID), F32),
            jax.ShapeDtypeStruct((3, 16, CMID), F32),
            jax.ShapeDtypeStruct((16, LAT), F32),
        ),
        in_specs=[vmem, vmem, vmem],
        out_specs=(hbm, vmem, vmem, vmem),
        scratch_shapes=[dma(())],
        compiler_params=pltpu.CompilerParams(vmem_limit_bytes=8 * 1024 * 1024),
    )(raw, sums, args[5])
    return (
        out.reshape(1, FR * NT, 8, CIN),
        space.reshape(3, 3, 8, CMID).transpose(2, 0, 1, 3),
        time.transpose(1, 0, 2),
        projg,
    )


def solution(mesh):
    placed = (
        P("clip", "tm", None, None, None),
        P("clip", "tm", None, None, None),
        P("clip", "tm", None, None, None),
        P(),
        P(),
        P(),
        P("clip", "tm", None, None),
        P("clip", "tm", None, None, None),
        P(),
    )
    return jax.shard_map(
        per_device,
        mesh=mesh,
        in_specs=placed,
        out_specs=(
            P("clip", None, "tm", None),
            P("tm", None, None, None),
            P("tm", None, None),
            P("tm", None),
        ),
        check_vma=False,
    )
```

```python
import jax
import jax.numpy as jnp
from jax import lax
from jax.experimental import pallas as pl
from jax.experimental.pallas import tpu as pltpu
from jax.sharding import PartitionSpec as P

MESH = pl.DeviceIdType.MESH
F32 = jnp.float32
BF16 = jnp.bfloat16
I32 = jnp.int32

NZ, NY, NX, NC = 8, 4, 4, 2
NT, NG = NZ * NY, NX * NC
FR, CELLS, CIN, CMID, LAT = 4, 256, 256, 512, 18
ROWS = FR * CELLS
PAIR = 2 * CELLS
SCALE = 1.0 / 512.0

NT_DIMS = (((1,), (1,)), ((), ()))
TN_DIMS = (((0,), (0,)), ((), ()))


def iota(shape, dim):
    return lax.broadcasted_iota(I32, shape, dim)


def ones_where(cond):
    return jnp.where(cond, 1.0, 0.0).astype(BF16)


def dot(a, b):
    return jnp.dot(a, b, preferred_element_type=F32)


def dot_nt(a, b):
    return lax.dot_general(a, b, NT_DIMS, preferred_element_type=F32)


def dot_tn(a, b):
    return lax.dot_general(a, b, TN_DIMS, preferred_element_type=F32)


def kernel(
    x_hbm, pre_hbm, t_hbm, ws_hbm, wt_hbm, pj_hbm, codes_hbm, cot_hbm, len_hbm,
    out_hbm, ra,
    x_v, pre_v, t_v, ws_v, wt_v, pj_v, codes_v, cot_v, len_ref,
    p3_v, gz_v, zc_v, mt_v, act_v, slope_v, g3_v, xt_v,
    halo_s, halo_r, ab_v,
    pw1, pw2, rc1, rc2,
    rel1, rel2, sum1, sum2, fin1, fin2,
    last1, last2, got1, got2, zs, rz,
    in_sem, halo_ss, halo_rs, a2a_ss, a2a_rs,
    core_ss, core_rs, x_ss, x_rs, y_ss, y_rs, z_ss, z_rs, g_ss, g_rs,
):
    tm = lax.axis_index("tm")
    clip = lax.axis_index("clip")
    z, y = tm // NY, tm % NY
    x, core = clip // NC, clip % NC

    def load(src, dst, i):
        copy = pltpu.make_async_copy(src, dst, in_sem.at[i])
        copy.start()
        return copy

    ld_pj = load(pj_hbm, pj_v, 0)
    ld_t0 = load(t_hbm.at[pl.ds(0, PAIR)], t_v.at[pl.ds(0, PAIR)], 1)
    ld_cd = load(codes_hbm, codes_v, 2)
    ld_ct = load(cot_hbm, cot_v, 3)
    ld_len = load(len_hbm, len_ref, 9)
    ld_t1 = load(t_hbm.at[pl.ds(PAIR, PAIR)], t_v.at[pl.ds(PAIR, PAIR)], 4)
    ld_wt = load(wt_hbm, wt_v, 5)
    ld_pre = load(pre_hbm, pre_v, 6)
    ld_x = load(x_hbm, x_v, 7)
    ld_ws = load(ws_hbm, ws_v, 8)

    barrier = pltpu.get_barrier_semaphore()

    @pl.loop(1, NT)
    def _(d):
        pl.semaphore_signal(
            barrier, inc=1, device_id=(lax.rem(tm + d, NT), clip), device_id_type=MESH
        )

    @pl.loop(1, NG)
    def _(d):
        pl.semaphore_signal(
            barrier, inc=1, device_id=(tm, lax.rem(clip + d, NG)), device_id_type=MESH
        )

    ld_pj.wait()
    row_l = iota((128, LAT), 0) % 32
    rep = ones_where(row_l == iota((128, LAT), 1))
    p3_v[...] = dot(rep, pj_v[...]).astype(BF16)

    rep_t = ones_where(iota((LAT, 128), 0) == iota((LAT, 128), 1) % 32)
    lane = iota((PAIR, 128), 1)
    lane_l = lane % 32
    row_id = iota((PAIR, 128), 0)
    spread = ones_where(iota((PAIR, 32), 0) // 16 == iota((PAIR, 32), 1))
    pick = ones_where(
        (iota((128, 128), 0) // 16 == (iota((128, 128), 1) % 32) // 6)
        & (iota((128, 128), 1) % 32 < LAT)
    )
    ld_len.wait()
    clip_len = len_ref[clip]

    def latents(fp):
        rows = pl.ds(fp * PAIR, PAIR)
        lat = dot_nt(t_v[rows, :], p3_v[...])
        cot = dot(cot_v[rows, :], rep_t)
        cd = codes_v[pl.ds(fp * 32, 32), :]
        packed = jnp.zeros((32, 128), F32)
        for piece in range(3):
            part = ((cd >> (6 * piece)) & 63).astype(F32).astype(BF16)
            place = ones_where(iota((16, 128), 1) == iota((16, 128), 0) + 16 * piece)
            packed = packed + dot(part, place)
        wide = dot(spread, packed.astype(BF16))
        own = jnp.where((lane < 48) & (lane % 16 == row_id % 16), wide, 0.0)
        six = dot(own.astype(BF16), pick).astype(I32)
        bit = (six >> (lane_l % 6)) & 1
        target = (2 * bit - 1).astype(F32)
        frame = tm * FR + fp * 2 + row_id // CELLS
        keep = (frame < clip_len) & (lane_l < LAT)
        grad = jnp.where(keep, cot + 0.5 * (lat - target), 0.0)
        gz_v[rows, :] = grad.astype(BF16)

    ld_t0.wait()
    ld_cd.wait()
    ld_ct.wait()
    latents(0)

    group = iota((CELLS, 128), 1) // 32

    def gz(f):
        return gz_v[f * CELLS : (f + 1) * CELLS, :].astype(F32)

    halo_s[...] = jnp.where(
        group == 0, 0.0, jnp.where(group == 2, gz(1), gz(0))
    ).astype(BF16)
    pl.semaphore_wait(barrier, NT - 1 + NG - 1)
    halo = pltpu.make_async_remote_copy(
        src_ref=halo_s, dst_ref=halo_r, send_sem=halo_ss, recv_sem=halo_rs,
        device_id=(lax.rem(tm + NT - 1, NT), clip), device_id_type=MESH,
    )
    halo.start()

    ld_t1.wait()
    latents(1)
    zc_v[0:CELLS, :] = jnp.where(
        group == 0, gz(0), jnp.where(group == 1, gz(1), jnp.where(group == 2, gz(2), 0.0))
    ).astype(BF16)
    zc_v[CELLS:PAIR, :] = jnp.where(
        group == 0, gz(1), jnp.where(group == 1, gz(2), jnp.where(group == 2, gz(3), 0.0))
    ).astype(BF16)

    ld_wt.wait()
    lane_g = iota((CMID, 128), 1) // 32
    fold = dot_nt(wt_v[2], p3_v[...])
    for k in range(2):
        fold = jnp.where(lane_g == k, dot_nt(wt_v[k], p3_v[...]), fold)
    mt_v[...] = fold.astype(BF16)

    ld_pre.wait()

    @pl.loop(0, ROWS // 64)
    def _(i):
        rows = pl.ds(pl.multiple_of(i * 64, 64), 64)
        v = pre_v[rows, :].astype(F32)
        s = 0.5 * jnp.tanh(0.5 * v) + 0.5
        a = v * s
        act_v[rows, :] = a.astype(BF16)
        slope_v[rows, :] = s + a * (1.0 - s)

    zero16 = jnp.zeros((16, CMID), BF16)

    def grad_pre(f):
        lo, hi = f * CELLS, (f + 1) * CELLS
        g = (dot_nt(zc_v[lo:hi, :], mt_v[...]) * slope_v[lo:hi, :]).astype(BF16)
        g3_v[1, lo:hi, :] = g
        g3_v[0, lo : hi - 16, :] = g[16:]
        g3_v[0, hi - 16 : hi, :] = zero16
        g3_v[2, lo + 16 : hi, :] = g[: CELLS - 16]
        g3_v[2, lo : lo + 16, :] = zero16

    row_p = iota((PAIR, CIN), 0) % 16

    def grad_x(fp):
        rows = slice(fp * PAIR, (fp + 1) * PAIR)
        back = []
        for b in range(3):
            acc = dot_nt(g3_v[0, rows, :], ws_v[b])
            for a in range(1, 3):
                acc = acc + dot_nt(g3_v[a, rows, :], ws_v[3 * a + b])
            back.append(acc)
        g = (
            back[1]
            + jnp.where(row_p != 15, pltpu.roll(back[0], PAIR - 1, 0), 0.0)
            + jnp.where(row_p != 0, pltpu.roll(back[2], 1, 0), 0.0)
        )
        for t in range(NT):
            both = jnp.concatenate(
                [g[8 * t : 8 * t + 8], g[CELLS + 8 * t : CELLS + 8 * t + 8]], axis=0
            )
            ab_v[t, fp] = both.astype(BF16)

    def send_x(fp):
        @pl.loop(1, NT)
        def _(d):
            to = lax.rem(z + d % NZ, NZ) * NY + lax.rem(y + d // NZ, NY)
            pltpu.make_async_remote_copy(
                src_ref=ab_v.at[to, fp], dst_ref=out_hbm.at[2 * tm + fp],
                send_sem=a2a_ss, recv_sem=a2a_rs,
                device_id=(to, clip), device_id_type=MESH,
            ).start()

        pltpu.make_async_copy(ab_v.at[tm, fp], out_hbm.at[2 * tm + fp], a2a_rs).start()

    grad_pre(0)
    grad_pre(1)

    ld_x.wait()
    r = iota((CIN, CIN), 0)
    c = iota((CIN, CIN), 1)
    perm = ones_where(
        c == (r // 16) % 4 * 64 + (r // 8) % 2 * 32 + r // 64 * 8 + r % 8
    )
    shift_lo = ones_where((r == c - 1) & (c % 16 != 0))
    shift_hi = ones_where((r == c + 1) & (c % 16 != 15))
    for f in range(FR):
        lo, hi = f * CELLS, (f + 1) * CELLS
        xt = dot_nt(perm, x_v[lo:hi, :]).astype(BF16)
        xt_v[256:512, lo:hi] = xt
        xt_v[0:256, lo:hi] = dot(xt, shift_lo).astype(BF16)
        xt_v[512:768, lo:hi] = dot(xt, shift_hi).astype(BF16)

    halo.wait_recv()
    ahead = jnp.where(tm == NT - 1, 0.0, halo_r[...].astype(F32))
    zc_v[PAIR : PAIR + CELLS, :] = jnp.where(
        group == 0, gz(2), jnp.where(group == 1, gz(3), jnp.where(group == 3, ahead, 0.0))
    ).astype(BF16)
    zc_v[PAIR + CELLS :, :] = jnp.where(
        group == 0, gz(3), jnp.where(group == 3, 0.0, ahead)
    ).astype(BF16)
    grad_pre(2)
    grad_pre(3)

    def space(a, half):
        cols = pl.ds(pl.multiple_of(half * 256, 256), 256)
        acc = dot(xt_v[...], g3_v[a, :, cols])
        for b in range(3):
            for lb in range(2):
                block = acc[256 * b : 256 * b + 256, 128 * lb : 128 * lb + 128].astype(BF16)
                if a < 2:
                    i = 6 * a + 2 * b + lb
                    pw1[half, i // 3, i % 3] = block
                else:
                    for yy in range(NY):
                        pw2[half, 2 * b + lb, yy] = block[64 * yy : 64 * yy + 64]

    def factors():
        gt = dot_tn(zc_v[...], act_v[...])
        pt = dot_tn(gz_v[...], t_v[...])
        q_t = jnp.concatenate([gt[0:64], gt[64:96] + gt[96:128], pt[96:128]], axis=0)
        q = q_t.T
        for cc in range(NC):
            for yy in range(NY):
                for zp in range(NZ // 2):
                    lo = 16 * (2 * zp * NY + yy) + 8 * cc
                    hi = 16 * ((2 * zp + 1) * NY + yy) + 8 * cc
                    tile = jnp.concatenate([q[lo : lo + 8], q[hi : hi + 8]], axis=0).astype(BF16)
                    pw2[cc, 6, yy, 16 * zp : 16 * zp + 16, :] = tile
                    pw2[cc, 7, yy, 16 * zp : 16 * zp + 16, :] = tile

    other = 1 - core

    def core_copy(src, dst, i):
        return pltpu.make_async_remote_copy(
            src_ref=src, dst_ref=dst, send_sem=core_ss.at[i], recv_sem=core_rs.at[i],
            device_id=(tm, x * NC + other), device_id_type=MESH,
        )

    core_copies = (
        core_copy(pw1.at[other, pl.ds(0, 2)], rc1.at[pl.ds(0, 2)], 0),
        core_copy(pw1.at[other, pl.ds(2, 2)], rc1.at[pl.ds(2, 2)], 1),
        core_copy(pw2.at[other], rc2, 2),
    )
    space(0, other)
    core_copies[0].start()
    space(1, other)
    core_copies[1].start()
    factors()
    space(2, other)
    core_copies[2].start()
    for a in range(3):
        space(a, core)

    def x_copy(src, dst, to, i):
        return pltpu.make_async_remote_copy(
            src_ref=src, dst_ref=dst, send_sem=x_ss.at[i], recv_sem=x_rs.at[i],
            device_id=(tm, to * NC + core), device_id_type=MESH,
        )

    def y_copy(src, dst, to, i):
        return pltpu.make_async_remote_copy(
            src_ref=src, dst_ref=dst, send_sem=y_ss.at[i], recv_sem=y_rs.at[i],
            device_id=(z * NY + to, clip), device_id_type=MESH,
        )

    def plus(a, b):
        return (a.astype(F32) + b.astype(F32)).astype(BF16)

    def halves1(ref, *at):
        return [ref.at[(*at, slice(None), pl.ds(128 * h, 128))] for h in range(2)]

    def halves2(ref, *at):
        return [ref.at[(*at, pl.ds(4 * h, 4))] for h in range(2)]

    def add1(chunk):
        for s in range(3):
            sum1[chunk, s] = plus(pw1[core, chunk, s], rc1[chunk, s])

    def add2(chunk):
        for s in range(8):
            sum2[chunk, s] = plus(pw2[core, s, chunk], rc2[s, chunk])

    def first(me, copy, halves, add, rel, sm, fin):
        left, right, far = lax.rem(me + 3, 4), lax.rem(me + 1, 4), lax.rem(me + 2, 4)
        add(far)
        a, b = halves(sm, far)
        copies = [copy(a, rel.at[0], left, 0), copy(b, rel.at[1], right, 1)]
        copies[0].start()
        copies[1].start()
        add(left)
        copies.append(copy(halves(sm, left)[1], halves(fin, 1)[1], left, 2))
        copies[2].start()
        add(right)
        copies.append(copy(halves(sm, right)[0], halves(fin, 0)[0], right, 3))
        copies[3].start()
        add(me)
        return copies

    def second(me, copy, halves, relay, sm, fin, copies):
        left, right = lax.rem(me + 3, 4), lax.rem(me + 1, 4)
        copies[0].wait_recv()
        relay(left, 0)
        copies.append(copy(halves(sm, left)[0], halves(fin, 1)[0], left, 4))
        copies[4].start()
        copies[1].wait_recv()
        relay(right, 1)
        copies.append(copy(halves(sm, right)[1], halves(fin, 0)[1], right, 5))
        copies[5].start()

    def relay1(chunk, h):
        for s in range(3):
            rows = slice(128 * h, 128 * h + 128)
            sum1[chunk, s, rows] = plus(sum1[chunk, s, rows], rel1[h, s])

    def relay2(chunk, h):
        for s in range(4):
            sum2[chunk, 4 * h + s] = plus(sum2[chunk, 4 * h + s], rel2[h, s])

    core_copies[0].wait_recv()
    core_copies[1].wait_recv()
    copies1 = first(x, x_copy, halves1, add1, rel1, sum1, fin1)
    core_copies[2].wait_recv()
    copies2 = first(y, y_copy, halves2, add2, rel2, sum2, fin2)

    ld_ws.wait()
    grad_x(0)
    send_x(0)

    second(y, y_copy, halves2, relay2, sum2, fin2, copies2)
    second(x, x_copy, halves1, relay1, sum1, fin1, copies1)

    grad_x(1)
    send_x(1)

    for copy in copies2[2:]:
        copy.wait_recv()
    for s in range(8):
        last2[s] = (
            sum2[y, s].astype(F32) + fin2[0, s].astype(F32) + fin2[1, s].astype(F32)
        ).astype(BF16)
    for d in range(1, NX):
        to = lax.rem(x + d, NX)
        copy = x_copy(last2.at[pl.ds(2 * to, 2)], got2.at[d - 1], to, 5 + d)
        copy.start()
        copies2.append(copy)
    for copy in copies1[2:]:
        copy.wait_recv()
    for s in range(3):
        tot = sum1[x, s].astype(F32) + fin1[0, s].astype(F32) + fin1[1, s].astype(F32)
        tot = tot.astype(BF16)
        for yy in range(NY):
            last1[yy, s] = tot[64 * yy : 64 * yy + 64]
    for d in range(1, NY):
        to = lax.rem(y + d, NY)
        copy = y_copy(last1.at[to], got1.at[d - 1], to, 5 + d)
        copy.start()
        copies1.append(copy)
    for copy in copies2[6:] + copies1[6:]:
        copy.wait_recv()
    tots = []
    for s in range(5):
        tot = (last1[y, s] if s < 3 else last2[2 * x + s - 3]).astype(F32)
        for d in range(3):
            tot = tot + (got1[d, s] if s < 3 else got2[d, s - 3]).astype(F32)
        tots.append(tot)
    blank = jnp.zeros((8, 128), F32)
    for zz in range(NZ):
        eights = [tot[8 * zz : 8 * zz + 8] for tot in tots] + [blank]
        for i in range(3):
            zs[zz, 16 * i : 16 * i + 16] = jnp.concatenate(
                eights[2 * i : 2 * i + 2], axis=0
            ).astype(BF16)

    z_copies = []
    for d in range(1, NZ):
        to = lax.rem(z + d, NZ)
        copy = pltpu.make_async_remote_copy(
            src_ref=zs.at[to], dst_ref=rz.at[d - 1],
            send_sem=z_ss.at[d - 1], recv_sem=z_rs.at[d - 1],
            device_id=(to * NY + y, clip), device_id_type=MESH,
        )
        copy.start()
        z_copies.append(copy)
    for copy in z_copies:
        copy.wait_recv()
    tot = zs[z].astype(F32)
    for d in range(NZ - 1):
        tot = tot + rz[d].astype(F32)
    ra[core, x] = (tot * SCALE).astype(BF16)

    g_copies = []
    for d in (4, 5, 3, 2, 6, 7, 1):
        copy = pltpu.make_async_remote_copy(
            src_ref=ra.at[core, x], dst_ref=ra.at[core, x],
            send_sem=g_ss.at[d - 1], recv_sem=g_rs.at[d - 1],
            device_id=(tm, lax.rem(clip + d, NG)), device_id_type=MESH,
        )
        copy.start()
        g_copies.append(copy)
    for copy in g_copies:
        copy.wait_recv()

    halo.wait_send()
    for copy in [*core_copies, *copies1, *copies2, *z_copies, *g_copies]:
        copy.wait_send()
    sent = ab_v.at[pl.ds(0, NT - 1)]
    pltpu.make_async_copy(sent, sent, a2a_ss).wait()
    pltpu.make_async_copy(out_hbm, out_hbm, a2a_rs).wait()


def finish(raw, ra, pj_ref, out_hbm, space_ref, time_ref, proj_ref, sem):
    whole = pltpu.make_async_copy(raw, out_hbm, sem)
    whole.start()
    for cc in range(NC):
        for i in range(18):
            a, b, lb = i // 6, i // 2 % 3, i % 2
            if a < 2:
                xx, s = i // 3, i % 3
            else:
                xx, s = (i - 12) // 2, 3 + i % 2
            tile = ra[cc, xx, 16 * (s // 2) : 16 * (s // 2) + 16].astype(F32)
            lo = 256 * cc + 128 * lb
            space_ref[3 * a + b, :, lo : lo + 128] = tile[8 * (s % 2) : 8 * (s % 2) + 8]
    qs = jnp.concatenate([ra[cc, 3, 16:32].astype(F32)[8:16] for cc in range(NC)], axis=0)
    qs = qs.astype(BF16)
    for k in range(3):
        take = ones_where(iota((128, LAT), 0) == iota((128, LAT), 1) + 32 * k)
        time_ref[k] = dot(dot(qs, take).astype(BF16), pj_ref[...])
    take = ones_where(iota((128, LAT), 0) == iota((128, LAT), 1) + 96)
    proj_ref[...] = dot(qs, take)
    whole.wait()


def per_device(block_input, pre_act, time_out, w_space, w_time, proj, codes, cotan, lengths):
    args = (
        block_input.reshape(ROWS, CIN),
        pre_act.reshape(ROWS, CMID),
        time_out.reshape(ROWS, CMID),
        w_space.transpose(1, 2, 0, 3).reshape(9, CIN, CMID),
        w_time.transpose(1, 0, 2),
        proj.T,
        codes.reshape(FR * 16, 16),
        cotan.reshape(ROWS, LAT),
        lengths,
    )
    hbm = pl.BlockSpec(memory_space=pltpu.HBM)
    held = [pltpu.with_memory_space_constraint(a, pltpu.HBM) for a in args]
    vmem = pl.BlockSpec(memory_space=pltpu.VMEM)
    dma = pltpu.SemaphoreType.DMA
    v = pltpu.VMEM
    limit = 40 * 1024 * 1024
    raw, sums = pl.pallas_call(
        kernel,
        out_shape=(pltpu.VMEM((2 * NT, 16, CIN), BF16), pltpu.VMEM((NC, NX, 48, 128), BF16)),
        in_specs=[hbm] * 9,
        out_specs=(vmem, vmem),
        scratch_shapes=[
            v((ROWS, CIN), BF16), v((ROWS, CMID), BF16), v((ROWS, CMID), BF16),
            v((9, CIN, CMID), BF16), v((3, CMID, CMID), BF16), v((LAT, CMID), BF16),
            v((FR * 16, 16), I32), v((ROWS, LAT), BF16), pltpu.SMEM((NG,), I32),
            v((128, CMID), BF16), v((ROWS, 128), BF16), v((ROWS, 128), BF16),
            v((CMID, 128), BF16), v((ROWS, CMID), BF16), v((ROWS, CMID), F32),
            v((3, ROWS, CMID), BF16), v((768, ROWS), BF16),
            v((CELLS, 128), BF16), v((CELLS, 128), BF16), v((NT, 2, 16, CIN), BF16),
            v((NC, NX, 3, 256, 128), BF16), v((NC, 8, NY, 64, 128), BF16),
            v((NX, 3, 256, 128), BF16), v((8, NY, 64, 128), BF16),
            v((2, 3, 128, 128), BF16), v((2, 4, 64, 128), BF16),
            v((NX, 3, 256, 128), BF16), v((NY, 8, 64, 128), BF16),
            v((2, 3, 256, 128), BF16), v((2, 8, 64, 128), BF16),
            v((NY, 3, 64, 128), BF16), v((8, 64, 128), BF16),
            v((NY - 1, 3, 64, 128), BF16), v((NX - 1, 2, 64, 128), BF16),
            v((NZ, 48, 128), BF16), v((NZ - 1, 48, 128), BF16),
            dma((10,)), dma(()), dma(()), dma(()), dma(()),
            dma((3,)), dma((3,)), dma((9,)), dma((9,)), dma((9,)), dma((9,)),
            dma((NZ - 1,)), dma((NZ - 1,)), dma((NG - 1,)), dma((NG - 1,)),
        ],
        compiler_params=pltpu.CompilerParams(
            collective_id=0, has_side_effects=True, vmem_limit_bytes=limit
        ),
    )(*held)
    out, space, time, projg = pl.pallas_call(
        finish,
        out_shape=(
            jax.ShapeDtypeStruct((2 * NT, 16, CIN), BF16),
            jax.ShapeDtypeStruct((9, 8, CMID), F32),
            jax.ShapeDtypeStruct((3, 16, CMID), F32),
            jax.ShapeDtypeStruct((16, LAT), F32),
        ),
        in_specs=[vmem, vmem, vmem],
        out_specs=(hbm, vmem, vmem, vmem),
        scratch_shapes=[dma(())],
        compiler_params=pltpu.CompilerParams(vmem_limit_bytes=8 * 1024 * 1024),
    )(raw, sums, args[5])
    return (
        out.reshape(1, FR * NT, 8, CIN),
        space.reshape(3, 3, 8, CMID).transpose(2, 0, 1, 3),
        time.transpose(1, 0, 2),
        projg,
    )


def solution(mesh):
    placed = (
        P("clip", "tm", None, None, None),
        P("clip", "tm", None, None, None),
        P("clip", "tm", None, None, None),
        P(),
        P(),
        P(),
        P("clip", "tm", None, None),
        P("clip", "tm", None, None, None),
        P(),
    )
    return jax.shard_map(
        per_device,
        mesh=mesh,
        in_specs=placed,
        out_specs=(
            P("clip", None, "tm", None),
            P("tm", None, None, None),
            P("tm", None, None),
            P("tm", None),
        ),
        check_vma=False,
    )
```
